32 devices in a mesh: gx: 8 (over z, x), gy: 4 (over y, core).
Axes of the slice: x: 2, y: 2, z: 4, core: 2. Of those that a mesh axis runs over, the one named last changes fastest.
Arguments:
- orbitals: float32 [32, 64, 32, 128], P(None, 'gx', 'gy'), may hold values from -340 to 340
- potential: float32 [64, 32, 128], P('gx', 'gy'), may hold values from -3 to 1
Outputs:
- orthonormal: float32 [32, 64, 32, 128], P(None, 'gx', 'gy')
- rfactor: float32 [32, 32], replicated
The draws below stay inside these ranges and needn't reach their ends.
All inputs are finite; a program needn't handle non-finite values.
Results may differ from the reference program's by a relative error of at most 0.0003.
Values sent between devices are 32-bit elements; how exact they have to be, the bound alone decides.
A program may use at most 128 MiB of HBM per device.

```python
import math
import jax
import jax.numpy as jnp
from jax import lax

NORB = 32
DEGREE = 3
CZ = 128
NX = 64
NY = 32
N_GX = 8
N_GY = 4


def draw_orbitals(key, part):
    subkeys = jax.random.split(key, 3)
    full_shape = (NORB, NX, NY, CZ)
    along_x = 1.0 + 2.0 * jnp.arange(NX, dtype=jnp.float32)[:, None, None] / max(NX - 1, 1)
    cell_scale = jnp.exp(jax.random.uniform(subkeys[1], (NX, NY, CZ), minval=math.log(0.3), maxval=math.log(3.0)))
    orbital_scale = jnp.exp(jax.random.uniform(subkeys[2], (NORB, 1, 1, 1), minval=math.log(0.3), maxval=math.log(3.0)))
    sample_values = jnp.clip(jax.random.normal(subkeys[0], full_shape), -6.0, 6.0)
    envelope = cell_scale * along_x
    return (sample_values * envelope[None] * orbital_scale).astype(jnp.float32)


def block_scale(own_key, shape, pieces, low, top_value):
    factor_of = 1.0
    for position, shards_of in pieces:
        steps = jax.random.uniform(jax.random.fold_in(jax.random.fold_in(own_key, 6), position), (shards_of,), jnp.float32, low / len(pieces), top_value / len(pieces))
        factor_of = factor_of * jnp.repeat(jnp.exp(steps), shape[position] // shards_of).reshape((-1,) + (1,) * (len(shape) - 1 - position))
    return factor_of


def setup_inputs(seed: int = 0) -> dict:
    key_of = jax.random.split(jax.random.key(seed), 3)
    return {
        "orbitals": draw_orbitals(jax.random.fold_in(key_of[2], 71), 0),
        "potential": jnp.clip(-3.0 + 4.0 * jax.random.uniform(key_of[1], (NX, NY, CZ), jnp.float32) ** block_scale(key_of[1], (NX, NY, CZ), ((0, 8), (1, 4)), -0.2, 0.2), -3.0, 1.0),
    }


stencil_weights = (-5369.0 / 1800.0, 12.0 / 7.0, -15.0 / 56.0, 10.0 / 189.0, -1.0 / 112.0, 2.0 / 1925.0, -1.0 / 16632.0)
grid_spacing = 0.5
filter_low = 4.0
filter_high = 46.0

def scaled_apply(orbital_field, potential):
    laplace = 3.0 * stencil_weights[0] * orbital_field
    for offset in range(1, 7):
        for axis_pos in range(3):
            laplace = laplace + stencil_weights[offset] * (jnp.roll(orbital_field, offset, axis_pos) + jnp.roll(orbital_field, -offset, axis_pos))
    applied = -0.5 / grid_spacing ** 2 * laplace + potential * orbital_field
    centre_shift = 0.5 * (filter_high + filter_low)
    half_width = 0.5 * (filter_high - filter_low)
    return (applied - centre_shift * orbital_field) / half_width

def reference(orbitals, potential):

    def filter_one(orbital_field):
        previous = orbital_field
        current = scaled_apply(orbital_field, potential)
        for degree_step in range(DEGREE - 1):
            following = 2.0 * scaled_apply(current, potential) - previous
            previous, current = (current, following)
        return current
    filtered = lax.map(filter_one, orbitals)
    cell_count = NX * NY * CZ
    matrix = filtered.reshape(NORB, cell_count)
    block_count = N_GX * N_GY
    blocks = matrix.reshape(NORB, block_count, cell_count // block_count).transpose(1, 2, 0)
    partial_r = lax.map(lambda block_rows: jnp.linalg.qr(block_rows, mode='r'), blocks)
    combined = jnp.linalg.qr(partial_r.reshape(block_count * NORB, NORB), mode='r')
    signs = jnp.where(jnp.diagonal(combined) >= 0, 1.0, -1.0).astype(combined.dtype)
    rfactor = combined * signs[:, None] / math.sqrt(cell_count)
    basis_rows = jax.scipy.linalg.solve_triangular(rfactor.T, matrix, lower=True)
    return (basis_rows.reshape(NORB, NX, NY, CZ), rfactor)
```

```python
import functools
import numpy as np
import jax
import jax.numpy as jnp
from jax import lax
from jax.experimental import pallas as pl
from jax.experimental.pallas import tpu as pltpu
from jax.sharding import PartitionSpec as P

DEGREE = 3
REACH = 6
stencil_weights = (
    -5369.0 / 1800.0,
    12.0 / 7.0,
    -15.0 / 56.0,
    10.0 / 189.0,
    -1.0 / 112.0,
    2.0 / 1925.0,
    -1.0 / 16632.0,
)
grid_spacing = 0.5
filter_low = 4.0
filter_high = 46.0
centre_shift = 0.5 * (filter_high + filter_low)
half_width = 0.5 * (filter_high - filter_low)
scale = -0.5 / grid_spacing**2 / half_width
side_weights = tuple(scale * w for w in stencil_weights)
highest = lax.Precision.HIGHEST
MESH = pl.DeviceIdType.MESH
CHUNK = 4


def circulant(size):
    matrix = np.zeros((size, size), np.float64)
    for offset in range(1, REACH + 1):
        for i in range(size):
            matrix[i, (i + offset) % size] += side_weights[offset]
            matrix[i, (i - offset) % size] += side_weights[offset]
    return matrix


def place(rows, n_gy):
    gx, gy = lax.axis_index("gx"), lax.axis_index("gy")
    inner = lax.rem(gx, rows)
    first = gx - inner
    return first, inner, gy, inner * n_gy + gy


def greet(first, member, count, n_gy):
    barrier = pltpu.get_barrier_semaphore()
    for k in range(1, count):
        t = lax.rem(member + k, count)
        pl.semaphore_signal(
            barrier, inc=1, device_id=(first + t // n_gy, lax.rem(t, n_gy)), device_id_type=MESH
        )
    pl.semaphore_wait(barrier, count - 1)


def far_first(count):
    return sorted(range(1, count), key=lambda k: -min(k, count - k))


def spread_kernel(rows, n_gy, orb, pot, field, allpot, send, recv, psend, precv, own):
    count = rows * n_gy
    bx, by = pot.shape[0], pot.shape[1]
    first, inner, gy, member = place(rows, n_gy)
    gx_bits, gy_bits = rows.bit_length() - 1, n_gy.bit_length() - 1
    bits = gx_bits + gy_bits
    mine = [lax.rem(member // (1 << (bits - 1 - b)), 2) for b in range(bits)]

    def region(done):
        index = [slice(None) if b < done else mine[b] for b in range(bits)]
        return allpot.at[tuple(index[:gx_bits]) + (slice(None),) + tuple(index[gx_bits:])]

    keep = pltpu.make_async_copy(
        orb.at[member], field.at[pl.ds(inner * bx, bx), pl.ds(gy * by, by)], own.at[0]
    )
    keep_pot = pltpu.make_async_copy(pot, region(0), own.at[1])
    keep.start()
    keep_pot.start()
    greet(first, member, count, n_gy)
    keep_pot.wait()

    order = far_first(count)
    copies = []
    per = -(-len(order) // max(bits, 1))
    for b in range(bits):
        stride = 1 << (bits - 1 - b)
        t = member + stride * (1 - 2 * mine[b])
        hop = pltpu.make_async_remote_copy(
            region(b),
            region(b),
            psend.at[b],
            precv.at[b],
            device_id=(first + t // n_gy, lax.rem(t, n_gy)),
            device_id_type=MESH,
        )
        hop.start()
        for k in order[b * per : (b + 1) * per]:
            t = lax.rem(member + k, count)
            copy = pltpu.make_async_remote_copy(
                orb.at[t],
                field.at[pl.ds(inner * bx, bx), pl.ds(gy * by, by)],
                send.at[k],
                recv.at[k],
                device_id=(first + t // n_gy, lax.rem(t, n_gy)),
                device_id_type=MESH,
            )
            copy.start()
            copies.append(copy)
        hop.wait()
    for copy in copies:
        copy.wait()
    keep.wait()


def return_kernel(rows, n_gy, field, out, send, recv, own):
    count = rows * n_gy
    bx, by = out.shape[1], out.shape[2]
    first, inner, gy, member = place(rows, n_gy)

    def part(t):
        return field.at[pl.ds((t // n_gy) * bx, bx), pl.ds(lax.rem(t, n_gy) * by, by)]

    keep = pltpu.make_async_copy(part(member), out.at[member], own)
    keep.start()
    greet(first, member, count, n_gy)
    copies = []
    for k in far_first(count):
        t = lax.rem(member + k, count)
        copy = pltpu.make_async_remote_copy(
            part(t),
            out.at[member],
            send.at[k],
            recv.at[k],
            device_id=(first + t // n_gy, lax.rem(t, n_gy)),
            device_id_type=MESH,
        )
        copy.start()
        copies.append(copy)
    for copy in copies:
        copy.wait()
    keep.wait()


def filter_kernel(extent, halo, field, pot, cy, cz, out, first_buf, second_buf):
    ny, nz = field.shape[1], field.shape[2]
    periodic = halo == 0
    origin = REACH if periodic else halo
    total = extent + 2 * origin

    def wrap(buf):
        if periodic:
            buf[0:REACH] = buf[extent : extent + REACH]
            buf[extent + REACH : total] = buf[REACH : 2 * REACH]

    if periodic:
        first_buf[REACH : REACH + extent] = field[...]
        wrap(first_buf)
    else:
        first_buf[...] = field[...]

    def apply(src, dst, dst_origin, prev, low, high):
        def body(i, carry):
            at = low + i * CHUNK
            here = origin + at
            centre = src[pl.ds(here, CHUNK)]
            flat = centre.reshape(CHUNK * ny, nz)
            lines = jnp.dot(flat, cz[...], precision=highest, preferred_element_type=jnp.float32)
            lines += jnp.dot(cy[...], flat, precision=highest, preferred_element_type=jnp.float32)
            diag = (pot[pl.ds(halo + at, CHUNK)] - centre_shift) * (1.0 / half_width)
            acc = (diag + 3.0 * side_weights[0]) * centre
            for offset in range(1, REACH + 1):
                acc += side_weights[offset] * (
                    src[pl.ds(here + offset, CHUNK)] + src[pl.ds(here - offset, CHUNK)]
                )
            acc += lines.reshape(CHUNK, ny, nz)
            if prev is not None:
                acc = 2.0 * acc - prev[pl.ds(here, CHUNK)]
            dst[pl.ds(dst_origin + at, CHUNK)] = acc
            return carry

        lax.fori_loop(0, (high - low) // CHUNK, body, 0)

    def margin(step):
        return 0 if periodic else REACH * (DEGREE - step)

    bufs = (first_buf, second_buf)
    for step in range(1, DEGREE + 1):
        src, other = bufs[(step - 1) % 2], bufs[step % 2]
        last = step == DEGREE
        m = margin(step)
        apply(
            src,
            out if last else other,
            0 if last else origin,
            None if step == 1 else other,
            -m,
            extent + m,
        )
        if not last:
            wrap(other)


def factor_kernel(n_gx, n_gy, gram, rfac, inverse, ybuf, xbuf, ysend, yrecv, xsend, xrecv):
    gx, gy = lax.axis_index("gx"), lax.axis_index("gy")
    norb = gram.shape[0]
    barrier = pltpu.get_barrier_semaphore()
    for k in range(1, n_gy):
        pl.semaphore_signal(
            barrier, inc=1, device_id=(gx, lax.rem(gy + k, n_gy)), device_id_type=MESH
        )
    for k in range(1, n_gx):
        pl.semaphore_signal(
            barrier, inc=1, device_id=(lax.rem(gx + k, n_gx), gy), device_id_type=MESH
        )
    pl.semaphore_wait(barrier, n_gy + n_gx - 2)

    ybuf[gy] = gram[...]
    copies = []
    for k in range(1, n_gy):
        copy = pltpu.make_async_remote_copy(
            ybuf.at[gy],
            ybuf.at[gy],
            ysend.at[k],
            yrecv.at[k],
            device_id=(gx, lax.rem(gy + k, n_gy)),
            device_id_type=MESH,
        )
        copy.start()
        copies.append(copy)
    for copy in copies:
        copy.wait()
    part = ybuf[0]
    for s in range(1, n_gy):
        part = part + ybuf[s]
    xbuf[gx] = part
    copies = []
    for k in range(1, n_gx):
        copy = pltpu.make_async_remote_copy(
            xbuf.at[gx],
            xbuf.at[gx],
            xsend.at[k],
            xrecv.at[k],
            device_id=(lax.rem(gx + k, n_gx), gy),
            device_id_type=MESH,
        )
        copy.start()
        copies.append(copy)
    for copy in copies:
        copy.wait()
    whole = xbuf[0]
    for s in range(1, n_gx):
        whole = whole + xbuf[s]

    row = lax.broadcasted_iota(jnp.int32, (norb, 128), 0)
    col = lax.broadcasted_iota(jnp.int32, (norb, 128), 1)
    table = jnp.where(col == row + norb, 1.0, whole)
    for k in range(norb):
        pivot_row = table[k : k + 1, :]
        root = lax.rsqrt(table[k : k + 1, k : k + 1])
        pivot_row = pivot_row * root
        column = table[:, k : k + 1] * root
        table = jnp.where(
            row == k, pivot_row, jnp.where(row > k, table - column * pivot_row, table)
        )
    upper = table[:, :norb]
    rfac[...] = jnp.where(row[:, :norb] <= col[:, :norb], upper, 0.0)
    inverse[...] = table[:, norb : 2 * norb]


def per_device(n_gx, n_gy, orbitals, potential):
    norb, bx, by, nz = orbitals.shape
    rows = norb // n_gy
    groups = n_gx // rows
    extent, ny = rows * bx, n_gy * by
    f32 = jnp.float32
    anywhere = pl.BlockSpec(memory_space=pl.ANY)
    vmem = pl.BlockSpec(memory_space=pltpu.VMEM)
    dma = pltpu.SemaphoreType.DMA
    gx_bits, gy_bits = rows.bit_length() - 1, n_gy.bit_length() - 1
    bits = gx_bits + gy_bits
    pot_shape = (2,) * gx_bits + (bx,) + (2,) * gy_bits + (by, nz)

    field, allpot = pl.pallas_call(
        functools.partial(spread_kernel, rows, n_gy),
        out_shape=(
            jax.ShapeDtypeStruct((extent, ny, nz), f32),
            jax.ShapeDtypeStruct(pot_shape, f32),
        ),
        in_specs=[anywhere] * 2,
        out_specs=(anywhere, anywhere),
        scratch_shapes=[dma((norb,)), dma((norb,)), dma((bits,)), dma((bits,)), dma((2,))],
        compiler_params=pltpu.CompilerParams(collective_id=0, has_side_effects=True),
        name="spread",
    )(orbitals, potential)
    allpot = allpot.reshape(extent, ny, nz)

    halo = 0
    if groups > 1:
        halo = REACH * DEGREE
        up = [(i, (i + rows) % n_gx) for i in range(n_gx)]
        down = [(t, s) for s, t in up]

        def widen(block):
            low = lax.ppermute(block[extent - halo :], "gx", up)
            high = lax.ppermute(block[:halo], "gx", down)
            return jnp.concatenate([low, block, high], axis=0)

        field, allpot = widen(field), widen(allpot)

    pad = extent + 2 * (halo if groups > 1 else REACH)
    cy = jnp.asarray(np.kron(np.eye(CHUNK), circulant(ny)), f32)
    cz = jnp.asarray(circulant(nz), f32)
    filtered = pl.pallas_call(
        functools.partial(filter_kernel, extent, halo),
        out_shape=jax.ShapeDtypeStruct((extent, ny, nz), f32),
        in_specs=[vmem] * 4,
        out_specs=vmem,
        scratch_shapes=[pltpu.VMEM((pad, ny, nz), f32)] * 2,
        compiler_params=pltpu.CompilerParams(vmem_limit_bytes=24 << 20),
        name="filter",
    )(field, allpot, cy, cz)

    back = pl.pallas_call(
        functools.partial(return_kernel, rows, n_gy),
        out_shape=jax.ShapeDtypeStruct((norb, bx, by, nz), f32),
        in_specs=[anywhere],
        out_specs=anywhere,
        scratch_shapes=[dma((norb,)), dma((norb,)), dma],
        compiler_params=pltpu.CompilerParams(collective_id=1, has_side_effects=True),
        name="hand_back",
    )(filtered)

    matrix = back.reshape(norb, -1)
    cells = float(matrix.shape[1] * n_gx * n_gy)
    gram = jnp.dot(matrix, matrix.T, precision=highest) / cells
    gram = jnp.pad(gram, ((0, 0), (0, 128 - norb)))
    rfactor, inverse = pl.pallas_call(
        functools.partial(factor_kernel, n_gx, n_gy),
        out_shape=(jax.ShapeDtypeStruct((norb, norb), f32),) * 2,
        in_specs=[vmem],
        out_specs=(vmem, vmem),
        scratch_shapes=[
            pltpu.VMEM((n_gy, norb, 128), f32),
            pltpu.VMEM((n_gx, norb, 128), f32),
            dma((n_gy,)),
            dma((n_gy,)),
            dma((n_gx,)),
            dma((n_gx,)),
        ],
        compiler_params=pltpu.CompilerParams(collective_id=2, has_side_effects=True),
        name="factor",
    )(gram)
    final = jnp.dot(inverse, matrix, precision=highest)
    return (final.reshape(orbitals.shape), rfactor)


def solution(mesh):
    return jax.shard_map(
        functools.partial(per_device, mesh.shape["gx"], mesh.shape["gy"]),
        mesh=mesh,
        in_specs=(P(None, "gx", "gy", None), P("gx", "gy", None)),
        out_specs=(P(None, "gx", "gy", None), P()),
        check_vma=False,
    )
```

```python
import functools
import numpy as np
import jax
import jax.numpy as jnp
from jax import lax
from jax.experimental import pallas as pl
from jax.experimental.pallas import tpu as pltpu
from jax.sharding import PartitionSpec as P

DEGREE = 3
REACH = 6
stencil_weights = (
    -5369.0 / 1800.0,
    12.0 / 7.0,
    -15.0 / 56.0,
    10.0 / 189.0,
    -1.0 / 112.0,
    2.0 / 1925.0,
    -1.0 / 16632.0,
)
grid_spacing = 0.5
filter_low = 4.0
filter_high = 46.0
centre_shift = 0.5 * (filter_high + filter_low)
half_width = 0.5 * (filter_high - filter_low)
scale = -0.5 / grid_spacing**2 / half_width
side_weights = tuple(scale * w for w in stencil_weights)
MESH = pl.DeviceIdType.MESH


def circulant(size):
    matrix = np.zeros((size, size), np.float64)
    for offset in range(1, REACH + 1):
        for i in range(size):
            matrix[i, (i + offset) % size] += side_weights[offset]
            matrix[i, (i - offset) % size] += side_weights[offset]
    return matrix


def split_const(matrix):
    parts, rest = [], matrix
    for _ in range(3):
        part = rest.astype(jnp.bfloat16)
        parts.append(part)
        rest = rest - part.astype(np.float64)
    return parts


def split(value):
    high = value.astype(jnp.bfloat16)
    rest = value - high.astype(jnp.float32)
    mid = rest.astype(jnp.bfloat16)
    low = (rest - mid.astype(jnp.float32)).astype(jnp.bfloat16)
    return high, mid, low


def place(rows):
    gx, gy = lax.axis_index("gx"), lax.axis_index("gy")
    inner = lax.rem(gx, rows)
    return gx - inner, inner, gy


def steps_far_near(rows, n_gy):
    steps = sorted(range(rows), key=lambda j: -min(j, rows - j))
    pairs = [(j, d) for j in steps for d in range(n_gy) if (j, d) != (0, 0)]
    mixed = []
    while pairs:
        mixed.append(pairs.pop(0))
        if pairs:
            mixed.append(pairs.pop())
    return mixed


def greet(rows, n_gy):
    first, inner, gy = place(rows)
    barrier = pltpu.get_barrier_semaphore()
    for j in range(rows):
        for d in range(n_gy):
            if (j, d) != (0, 0):
                who = (first + lax.rem(inner + j, rows), lax.rem(gy + d, n_gy))
                pl.semaphore_signal(barrier, inc=1, device_id=who, device_id_type=MESH)
    pl.semaphore_wait(barrier, rows * n_gy - 1)


def spread(rows, n_gy, origin, orb, pot, field, allpot, send, recv, psend, precv, own):
    bx, by = pot.shape[0], pot.shape[1]
    first, inner, gy = place(rows)
    gx_bits, gy_bits = rows.bit_length() - 1, n_gy.bit_length() - 1
    bits = gx_bits + gy_bits
    member = inner * n_gy + gy
    mine = [lax.rem(member // (1 << (bits - 1 - b)), 2) for b in range(bits)]
    brick = field.at[
        pl.ds(origin + inner * bx, bx), pl.ds(pl.multiple_of(gy * by, by), by)
    ]

    def region(done):
        index = [slice(None) if b < done else mine[b] for b in range(bits)]
        return allpot.at[tuple(index[:gx_bits]) + (slice(None),) + tuple(index[gx_bits:])]

    keep = pltpu.make_async_copy(orb.at[member], brick, own.at[0])
    keep_pot = pltpu.make_async_copy(pot, region(0), own.at[1])
    keep.start()
    keep_pot.start()
    greet(rows, n_gy)
    keep_pot.wait()

    order = steps_far_near(rows, n_gy)
    copies = []
    per = -(-len(order) // max(bits, 1))
    for b in range(bits):
        stride = 1 << (bits - 1 - b)
        t = member + stride * (1 - 2 * mine[b])
        hop = pltpu.make_async_remote_copy(
            region(b),
            region(b),
            psend.at[b],
            precv.at[b],
            device_id=(first + t // n_gy, lax.rem(t, n_gy)),
            device_id_type=MESH,
        )
        hop.start()
        for j, d in order[b * per : (b + 1) * per]:
            tx, ty = lax.rem(inner + j, rows), lax.rem(gy + d, n_gy)
            copy = pltpu.make_async_remote_copy(
                orb.at[tx * n_gy + ty],
                brick,
                send.at[j * n_gy + d],
                recv.at[j * n_gy + d],
                device_id=(first + tx, ty),
                device_id_type=MESH,
            )
            copy.start()
            copies.append(copy)
        hop.wait()
    for copy in copies:
        copy.wait()
    keep.wait()


def send_block(rows, n_gy, origin, j, field, out, send, recv, own):
    bx, by = out.shape[1], out.shape[2]
    first, inner, gy = place(rows)
    member = inner * n_gy + gy
    tx = lax.rem(inner + j, rows)
    copies = []
    for d in range(n_gy):
        ty = lax.rem(gy + d, n_gy)
        part = field.at[
            pl.ds(origin + tx * bx, bx), pl.ds(pl.multiple_of(ty * by, by), by)
        ]
        if (j, d) == (0, 0):
            copy = pltpu.make_async_copy(part, out.at[member], own)
        else:
            copy = pltpu.make_async_remote_copy(
                part,
                out.at[member],
                send.at[j * n_gy + d],
                recv.at[j * n_gy + d],
                device_id=(first + tx, ty),
                device_id_type=MESH,
            )
        copy.start()
        copies.append(copy)
    return copies


def block_order(rows):
    steps = sorted(range(1, rows), key=lambda j: -min(j, rows - j))
    mixed = []
    while steps:
        mixed.append(steps.pop(0))
        if steps:
            mixed.append(steps.pop())
    return mixed + [0]


def apply_planes(src, here, count, pot_planes, cz, cy, dst, there, prev):
    ny, nz = src.shape[1], src.shape[2]
    group = cy.shape[0] // ny
    centre = src[pl.ds(here, count)]
    acc = ((pot_planes - centre_shift) * (1.0 / half_width) + 3.0 * side_weights[0]) * centre
    high, mid, low = split(centre.reshape(count * ny, nz))
    lines = jnp.dot(
        jnp.concatenate([high, mid, low, high, mid, high], axis=1),
        cz[...],
        preferred_element_type=jnp.float32,
    )
    across = []
    for g in range(count // group):
        rows = slice(g * group * ny, (g + 1) * group * ny)
        h, m, l = high[rows], mid[rows], low[rows]
        across.append(
            jnp.dot(
                cy[...],
                jnp.concatenate([h, m, l, h, m, h], axis=0),
                preferred_element_type=jnp.float32,
            )
        )
    lines = lines + jnp.concatenate(across, axis=0)
    for offset in range(1, REACH + 1):
        acc += side_weights[offset] * (
            src[pl.ds(here + offset, count)] + src[pl.ds(here - offset, count)]
        )
    acc += lines.reshape(count, ny, nz)
    if prev is not None:
        acc = 2.0 * acc - prev[pl.ds(here, count)]
    dst[pl.ds(there, count)] = acc


def whole_kernel(
    rows, n_gy, orb, pot, cy, cz, out,
    first_buf, second_buf, allpot, send, recv, psend, precv, own, bsend, brecv,
):
    bx, ny, nz = pot.shape[0], first_buf.shape[1], first_buf.shape[2]
    extent = rows * bx
    gx_bits = rows.bit_length() - 1
    spread(rows, n_gy, REACH, orb, pot, first_buf, allpot, send, recv, psend, precv, own)
    _, inner, _ = place(rows)

    def pot_block(block):
        index = tuple(lax.rem(block // (1 << (gx_bits - 1 - b)), 2) for b in range(gx_bits))
        return allpot[index].reshape(bx, ny, nz)

    def wrap(buf):
        buf[0:REACH] = buf[extent : extent + REACH]
        buf[extent + REACH : extent + 2 * REACH] = buf[REACH : 2 * REACH]

    bufs = (first_buf, second_buf)
    copies = []
    for step in range(1, DEGREE + 1):
        src, other = bufs[(step - 1) % 2], bufs[step % 2]
        wrap(src)
        prev = None if step == 1 else other
        if step < DEGREE:

            def body(block, carry, src=src, other=other, prev=prev):
                at = REACH + block * bx
                apply_planes(src, at, bx, pot_block(block), cz, cy, other, at, prev)
                return carry

            lax.fori_loop(0, rows, body, 0, unroll=True)
        else:
            for j in block_order(rows):
                block = lax.rem(inner + j, rows)
                at = REACH + block * bx
                apply_planes(src, at, bx, pot_block(block), cz, cy, other, at, prev)
                copies += send_block(
                    rows, n_gy, REACH, j, other, out, bsend, brecv, own.at[0]
                )
    for copy in copies:
        copy.wait()


def spread_kernel(rows, n_gy, orb, pot, field, allpot, send, recv, psend, precv, own):
    spread(rows, n_gy, 0, orb, pot, field, allpot, send, recv, psend, precv, own)


def return_kernel(rows, n_gy, field, out, send, recv, own):
    greet(rows, n_gy)
    copies = []
    for j in block_order(rows):
        copies += send_block(rows, n_gy, 0, j, field, out, send, recv, own)
    for copy in copies:
        copy.wait()


def filter_kernel(extent, field, pot, cy, cz, out, first_buf, second_buf):
    origin = REACH * DEGREE
    count = cy.shape[0] // field.shape[1]
    first_buf[...] = field[...]
    bufs = (first_buf, second_buf)
    for step in range(1, DEGREE + 1):
        src, other = bufs[(step - 1) % 2], bufs[step % 2]
        last = step == DEGREE
        margin = REACH * (DEGREE - step)
        prev = None if step == 1 else other
        dst, base = (out, 0) if last else (other, origin)

        def body(i, carry, src=src, dst=dst, base=base, prev=prev, margin=margin):
            at = i * count - margin
            planes = pot[pl.ds(origin + at, count)]
            apply_planes(src, origin + at, count, planes, cz, cy, dst, base + at, prev)
            return carry

        lax.fori_loop(0, (extent + 2 * margin) // count, body, 0)


def factor_kernel(
    n_gx, n_gy, cells, matrix, rfac, inverse, stack, ybuf, xbuf, ysend, yrecv, xsend, xrecv
):
    gx, gy = lax.axis_index("gx"), lax.axis_index("gy")
    norb = rfac.shape[0]
    nz = matrix.shape[1]
    lines = matrix.shape[0] // norb
    barrier = pltpu.get_barrier_semaphore()
    for k in range(1, n_gy):
        pl.semaphore_signal(
            barrier, inc=1, device_id=(gx, lax.rem(gy + k, n_gy)), device_id_type=MESH
        )
    for k in range(1, n_gx):
        pl.semaphore_signal(
            barrier, inc=1, device_id=(lax.rem(gx + k, n_gx), gy), device_id_type=MESH
        )

    for r in range(lines):
        for p, part in enumerate(split(matrix[pl.ds(r, norb, stride=lines)])):
            stack[p * norb : (p + 1) * norb, r * nz : (r + 1) * nz] = part
    square = lax.dot_general(
        stack[...], stack[...], (((1,), (1,)), ((), ())), preferred_element_type=jnp.float32
    )
    gram = None
    for p, q in ((2, 2), (1, 2), (2, 1), (0, 2), (2, 0), (1, 1), (0, 1), (1, 0), (0, 0)):
        term = square[p * norb : (p + 1) * norb, q * norb : (q + 1) * norb]
        gram = term if gram is None else gram + term
    gram = jnp.concatenate([gram / cells, jnp.zeros((norb, 128 - norb), jnp.float32)], axis=1)

    pl.semaphore_wait(barrier, n_gy + n_gx - 2)
    ybuf[gy] = gram
    copies = []
    for k in range(1, n_gy):
        copy = pltpu.make_async_remote_copy(
            ybuf.at[gy],
            ybuf.at[gy],
            ysend.at[k],
            yrecv.at[k],
            device_id=(gx, lax.rem(gy + k, n_gy)),
            device_id_type=MESH,
        )
        copy.start()
        copies.append(copy)
    for copy in copies:
        copy.wait()
    part = ybuf[0]
    for s in range(1, n_gy):
        part = part + ybuf[s]
    xbuf[gx] = part
    copies = []
    for k in range(1, n_gx):
        copy = pltpu.make_async_remote_copy(
            xbuf.at[gx],
            xbuf.at[gx],
            xsend.at[k],
            xrecv.at[k],
            device_id=(lax.rem(gx + k, n_gx), gy),
            device_id_type=MESH,
        )
        copy.start()
        copies.append(copy)
    for copy in copies:
        copy.wait()
    whole = xbuf[0]
    for s in range(1, n_gx):
        whole = whole + xbuf[s]

    row = lax.broadcasted_iota(jnp.int32, (norb, 128), 0)
    col = lax.broadcasted_iota(jnp.int32, (norb, 128), 1)
    table = jnp.where(col == row + norb, 1.0, whole)
    pivots = jnp.zeros((norb, 128), jnp.float32)
    for k in range(norb):
        pivot = table[k : k + 1, k : k + 1]
        pivots = jnp.where(row == k, pivot, pivots)
        ratio = jnp.where(row[:, :1] > k, table[:, k : k + 1] * (1.0 / pivot), 0.0)
        table = table - ratio * table[k : k + 1, :]
    table = table * lax.rsqrt(pivots)
    rfac[...] = jnp.where(row[:, :norb] <= col[:, :norb], table[:, :norb], 0.0)
    inverse[...] = table[:, norb : 2 * norb]


def mix_kernel(matrix, inverse, out):
    norb = inverse.shape[0]
    lines = matrix.shape[0] // norb
    nz = matrix.shape[1]
    h, m, l = split(inverse[...])
    left = jnp.concatenate([h, h, h, m, m, l], axis=1)
    for r in range(0, lines, 2):
        both = jnp.concatenate(
            [matrix[pl.ds(r + i, norb, stride=lines)] for i in range(2)], axis=1
        )
        h, m, l = split(both)
        mixed = jnp.dot(
            left,
            jnp.concatenate([h, m, l, h, m, h], axis=0),
            preferred_element_type=jnp.float32,
        )
        for i in range(2):
            out[pl.ds(r + i, norb, stride=lines)] = mixed[:, i * nz : (i + 1) * nz]


def per_device(n_gx, n_gy, orbitals, potential):
    norb, bx, by, nz = orbitals.shape
    rows = norb // n_gy
    groups = n_gx // rows
    extent, ny = rows * bx, n_gy * by
    f32 = jnp.float32
    anywhere = pl.BlockSpec(memory_space=pl.ANY)
    vmem = pl.BlockSpec(memory_space=pltpu.VMEM)
    dma = pltpu.SemaphoreType.DMA
    gx_bits, gy_bits = rows.bit_length() - 1, n_gy.bit_length() - 1
    bits = gx_bits + gy_bits
    pot_shape = (2,) * gx_bits + (bx,) + (2,) * gy_bits + (by, nz)
    spread_sems = [dma((norb,)), dma((norb,)), dma((bits,)), dma((bits,)), dma((2,))]
    brick_shape = jax.ShapeDtypeStruct((norb, bx, by, nz), f32)

    yh, ym, yl = split_const(np.kron(np.eye(4), circulant(ny)))
    cy = jnp.asarray(np.concatenate([yh, yh, yh, ym, ym, yl], axis=1))
    zh, zm, zl = split_const(circulant(nz))
    cz = jnp.asarray(np.concatenate([zh, zh, zh, zm, zm, zl], axis=0))

    if groups == 1:
        planes = extent + 2 * REACH
        back = pl.pallas_call(
            functools.partial(whole_kernel, rows, n_gy),
            out_shape=brick_shape,
            in_specs=[anywhere, anywhere, vmem, vmem],
            out_specs=vmem,
            scratch_shapes=[
                pltpu.VMEM((planes, ny, nz), f32),
                pltpu.VMEM((planes, ny, nz), f32),
                pltpu.VMEM(pot_shape, f32),
            ]
            + spread_sems
            + [dma((norb,)), dma((norb,))],
            compiler_params=pltpu.CompilerParams(
                collective_id=0, has_side_effects=True, vmem_limit_bytes=24 << 20
            ),
            name="spread_filter_return",
        )(orbitals, potential, cy, cz)
    else:
        field, allpot = pl.pallas_call(
            functools.partial(spread_kernel, rows, n_gy),
            out_shape=(
                jax.ShapeDtypeStruct((extent, ny, nz), f32),
                jax.ShapeDtypeStruct(pot_shape, f32),
            ),
            in_specs=[anywhere] * 2,
            out_specs=(anywhere, anywhere),
            scratch_shapes=spread_sems,
            compiler_params=pltpu.CompilerParams(collective_id=0, has_side_effects=True),
            name="spread",
        )(orbitals, potential)
        halo = REACH * DEGREE
        up = [(i, (i + rows) % n_gx) for i in range(n_gx)]
        down = [(t, s) for s, t in up]

        def widen(block):
            low = lax.ppermute(block[extent - halo :], "gx", up)
            high = lax.ppermute(block[:halo], "gx", down)
            return jnp.concatenate([low, block, high], axis=0)

        planes = extent + 2 * halo
        filtered = pl.pallas_call(
            functools.partial(filter_kernel, extent),
            out_shape=jax.ShapeDtypeStruct((extent, ny, nz), f32),
            in_specs=[vmem] * 4,
            out_specs=vmem,
            scratch_shapes=[pltpu.VMEM((planes, ny, nz), f32)] * 2,
            compiler_params=pltpu.CompilerParams(vmem_limit_bytes=24 << 20),
            name="filter",
        )(widen(field), widen(allpot.reshape(extent, ny, nz)), cy, cz)
        back = pl.pallas_call(
            functools.partial(return_kernel, rows, n_gy),
            out_shape=brick_shape,
            in_specs=[anywhere],
            out_specs=anywhere,
            scratch_shapes=[dma((norb,)), dma((norb,)), dma],
            compiler_params=pltpu.CompilerParams(collective_id=1, has_side_effects=True),
            name="hand_back",
        )(filtered)

    matrix = back.reshape(norb * bx * by, nz)
    cells = float(bx * by * nz * n_gx * n_gy)
    rfactor, inverse = pl.pallas_call(
        functools.partial(factor_kernel, n_gx, n_gy, cells),
        out_shape=(jax.ShapeDtypeStruct((norb, norb), f32),) * 2,
        in_specs=[vmem],
        out_specs=(vmem, vmem),
        scratch_shapes=[
            pltpu.VMEM((3 * norb, bx * by * nz), jnp.bfloat16),
            pltpu.VMEM((n_gy, norb, 128), f32),
            pltpu.VMEM((n_gx, norb, 128), f32),
            dma((n_gy,)),
            dma((n_gy,)),
            dma((n_gx,)),
            dma((n_gx,)),
        ],
        compiler_params=pltpu.CompilerParams(
            collective_id=2, has_side_effects=True, vmem_limit_bytes=24 << 20
        ),
        name="factor",
    )(matrix)
    final = pl.pallas_call(
        mix_kernel,
        out_shape=jax.ShapeDtypeStruct(matrix.shape, f32),
        in_specs=[vmem, vmem],
        out_specs=vmem,
        compiler_params=pltpu.CompilerParams(vmem_limit_bytes=24 << 20),
        name="mix",
    )(matrix, inverse)
    return (final.reshape(orbitals.shape), rfactor)


def solution(mesh):
    return jax.shard_map(
        functools.partial(per_device, mesh.shape["gx"], mesh.shape["gy"]),
        mesh=mesh,
        in_specs=(P(None, "gx", "gy", None), P("gx", "gy", None)),
        out_specs=(P(None, "gx", "gy", None), P()),
        check_vma=False,
    )
```

```python
import functools
import numpy as np
import jax
import jax.numpy as jnp
from jax import lax
from jax.experimental import pallas as pl
from jax.experimental.pallas import tpu as pltpu
from jax.sharding import PartitionSpec as P

DEGREE = 3
REACH = 6
stencil_weights = (
    -5369.0 / 1800.0,
    12.0 / 7.0,
    -15.0 / 56.0,
    10.0 / 189.0,
    -1.0 / 112.0,
    2.0 / 1925.0,
    -1.0 / 16632.0,
)
grid_spacing = 0.5
filter_low = 4.0
filter_high = 46.0
centre_shift = 0.5 * (filter_high + filter_low)
half_width = 0.5 * (filter_high - filter_low)
scale = -0.5 / grid_spacing**2 / half_width
side_weights = tuple(scale * w for w in stencil_weights)
MESH = pl.DeviceIdType.MESH


def circulant(size):
    matrix = np.zeros((size, size), np.float64)
    for offset in range(1, REACH + 1):
        for i in range(size):
            matrix[i, (i + offset) % size] += side_weights[offset]
            matrix[i, (i - offset) % size] += side_weights[offset]
    return matrix


def split_const(matrix):
    parts, rest = [], matrix
    for _ in range(3):
        part = rest.astype(jnp.bfloat16)
        parts.append(part)
        rest = rest - part.astype(np.float64)
    return parts


def split(value):
    high = value.astype(jnp.bfloat16)
    rest = value - high.astype(jnp.float32)
    mid = rest.astype(jnp.bfloat16)
    low = (rest - mid.astype(jnp.float32)).astype(jnp.bfloat16)
    return high, mid, low


def place(rows):
    gx, gy = lax.axis_index("gx"), lax.axis_index("gy")
    inner = lax.rem(gx, rows)
    return gx - inner, inner, gy


def steps_far_near(rows, n_gy):
    steps = sorted(range(rows), key=lambda j: -min(j, rows - j))
    pairs = [(j, d) for j in steps for d in range(n_gy) if (j, d) != (0, 0)]
    mixed = []
    while pairs:
        mixed.append(pairs.pop(0))
        if pairs:
            mixed.append(pairs.pop())
    return mixed


def greet(rows, n_gy):
    first, inner, gy = place(rows)
    barrier = pltpu.get_barrier_semaphore()
    for j in range(rows):
        for d in range(n_gy):
            if (j, d) != (0, 0):
                who = (first + lax.rem(inner + j, rows), lax.rem(gy + d, n_gy))
                pl.semaphore_signal(barrier, inc=1, device_id=who, device_id_type=MESH)
    pl.semaphore_wait(barrier, rows * n_gy - 1)


def spread(
    rows, n_gy, origin, orb, pot, field, allpot, send, recv, psend, precv, own, meanwhile=None
):
    bx, by = pot.shape[0], pot.shape[1]
    first, inner, gy = place(rows)
    gx_bits, gy_bits = rows.bit_length() - 1, n_gy.bit_length() - 1
    bits = gx_bits + gy_bits
    member = inner * n_gy + gy
    mine = [lax.rem(member // (1 << (bits - 1 - b)), 2) for b in range(bits)]
    brick = field.at[
        pl.ds(origin + inner * bx, bx), pl.ds(pl.multiple_of(gy * by, by), by)
    ]

    def region(done):
        index = [slice(None) if b in done else mine[b] for b in range(bits)]
        return allpot.at[tuple(index[:gx_bits]) + (slice(None),) + tuple(index[gx_bits:])]

    def hop(stage, bit, done):
        t = member + (1 << (bits - 1 - bit)) * (1 - 2 * mine[bit])
        return pltpu.make_async_remote_copy(
            region(done),
            region(done),
            psend.at[stage],
            precv.at[stage],
            device_id=(first + t // n_gy, lax.rem(t, n_gy)),
            device_id_type=MESH,
        )

    plain = list(range(bits))
    swapped = list(plain)
    if bits >= 3:
        swapped[bits - 3], swapped[bits - 2] = bits - 2, bits - 3
    odd = mine[bits - 1] == 1

    def on_hop(stage, act):
        if plain[: stage + 1] == swapped[: stage + 1] or stage == bits - 1:
            act(hop(stage, plain[stage], plain[:stage]))
        else:
            pl.when(jnp.logical_not(odd))(
                lambda: act(hop(stage, plain[stage], plain[:stage]))
            )
            pl.when(odd)(lambda: act(hop(stage, swapped[stage], swapped[:stage])))

    keep = pltpu.make_async_copy(orb.at[member], brick, own.at[0])
    keep_pot = pltpu.make_async_copy(pot, region([]), own.at[1])
    keep.start()
    keep_pot.start()
    greet(rows, n_gy)
    keep_pot.wait()

    order = steps_far_near(rows, n_gy)
    copies = []
    per = -(-len(order) // max(bits, 1))
    for b in range(bits):
        on_hop(b, lambda copy: copy.start())
        for j, d in order[b * per : (b + 1) * per]:
            tx, ty = lax.rem(inner + j, rows), lax.rem(gy + d, n_gy)
            copy = pltpu.make_async_remote_copy(
                orb.at[tx * n_gy + ty],
                brick,
                send.at[j * n_gy + d],
                recv.at[j * n_gy + d],
                device_id=(first + tx, ty),
                device_id_type=MESH,
            )
            copy.start()
            copies.append(copy)
        on_hop(b, lambda copy: copy.wait())
    if meanwhile is not None:
        meanwhile()
    for copy in copies:
        copy.wait()
    keep.wait()


def send_block(rows, n_gy, origin, j, field, out, send, recv, own):
    bx, by = out.shape[1], out.shape[2]
    first, inner, gy = place(rows)
    member = inner * n_gy + gy
    tx = lax.rem(inner + j, rows)
    copies = []
    for d in range(n_gy):
        ty = lax.rem(gy + d, n_gy)
        part = field.at[
            pl.ds(origin + tx * bx, bx), pl.ds(pl.multiple_of(ty * by, by), by)
        ]
        if (j, d) == (0, 0):
            copy = pltpu.make_async_copy(part, out.at[member], own)
        else:
            copy = pltpu.make_async_remote_copy(
                part,
                out.at[member],
                send.at[j * n_gy + d],
                recv.at[j * n_gy + d],
                device_id=(first + tx, ty),
                device_id_type=MESH,
            )
        copy.start()
        copies.append(copy)
    return copies


def block_order(rows):
    steps = sorted(range(1, rows), key=lambda j: -min(j, rows - j))
    mixed = []
    while steps:
        mixed.append(steps.pop(0))
        if steps:
            mixed.append(steps.pop())
    return mixed + [0]


def apply_planes(src, here, count, pot_planes, cz, cy, dst, there, prev):
    ny, nz = src.shape[1], src.shape[2]
    group = cy.shape[0] // ny
    centre = src[pl.ds(here, count)]
    acc = ((pot_planes - centre_shift) * (1.0 / half_width) + 3.0 * side_weights[0]) * centre
    high, mid, low = split(centre.reshape(count * ny, nz))
    lines = jnp.dot(
        jnp.concatenate([high, mid, low, high, mid, high], axis=1),
        cz[...],
        preferred_element_type=jnp.float32,
    )
    across = []
    for g in range(count // group):
        rows = slice(g * group * ny, (g + 1) * group * ny)
        h, m, l = high[rows], mid[rows], low[rows]
        across.append(
            jnp.dot(
                cy[...],
                jnp.concatenate([h, m, l, h, m, h], axis=0),
                preferred_element_type=jnp.float32,
            )
        )
    lines = lines + jnp.concatenate(across, axis=0)
    for offset in range(1, REACH + 1):
        acc += side_weights[offset] * (
            src[pl.ds(here + offset, count)] + src[pl.ds(here - offset, count)]
        )
    acc += lines.reshape(count, ny, nz)
    if prev is not None:
        acc = 2.0 * acc - prev[pl.ds(here, count)]
    dst[pl.ds(there, count)] = acc


def whole_kernel(
    rows, n_gy, orb, pot, cy_far, cz_far, out,
    cy_wide, cz_wide, cy, cz, first_buf, second_buf, allpot, send, recv, psend, precv, own, bsend, brecv,
):
    bx, ny, nz = pot.shape[0], first_buf.shape[1], first_buf.shape[2]
    extent = rows * bx
    gx_bits = rows.bit_length() - 1
    fetch = [
        pltpu.make_async_copy(cy_far, cy_wide, own.at[2]),
        pltpu.make_async_copy(cz_far, cz_wide, own.at[3]),
    ]
    for copy in fetch:
        copy.start()

    def fetched():
        for copy in fetch:
            copy.wait()
        cy[...] = cy_wide[...].astype(jnp.bfloat16)
        cz[...] = cz_wide[...].astype(jnp.bfloat16)

    spread(rows, n_gy, REACH, orb, pot, first_buf, allpot, send, recv, psend, precv, own,
           fetched)
    _, inner, _ = place(rows)

    def pot_block(block):
        index = tuple(lax.rem(block // (1 << (gx_bits - 1 - b)), 2) for b in range(gx_bits))
        return allpot[index].reshape(bx, ny, nz)

    def wrap(buf):
        buf[0:REACH] = buf[extent : extent + REACH]
        buf[extent + REACH : extent + 2 * REACH] = buf[REACH : 2 * REACH]

    bufs = (first_buf, second_buf)
    copies = []
    for step in range(1, DEGREE + 1):
        src, other = bufs[(step - 1) % 2], bufs[step % 2]
        wrap(src)
        prev = None if step == 1 else other
        if step < DEGREE:

            def body(block, carry, src=src, other=other, prev=prev):
                at = REACH + block * bx
                apply_planes(src, at, bx, pot_block(block), cz, cy, other, at, prev)
                return carry

            lax.fori_loop(0, rows, body, 0, unroll=True)
        else:
            for j in block_order(rows):
                block = lax.rem(inner + j, rows)
                at = REACH + block * bx
                apply_planes(src, at, bx, pot_block(block), cz, cy, other, at, prev)
                copies += send_block(
                    rows, n_gy, REACH, j, other, out, bsend, brecv, own.at[0]
                )
    for copy in copies:
        copy.wait()


def spread_kernel(rows, n_gy, orb, pot, field, allpot, send, recv, psend, precv, own):
    spread(rows, n_gy, 0, orb, pot, field, allpot, send, recv, psend, precv, own)


def return_kernel(rows, n_gy, field, out, send, recv, own):
    greet(rows, n_gy)
    copies = []
    for j in block_order(rows):
        copies += send_block(rows, n_gy, 0, j, field, out, send, recv, own)
    for copy in copies:
        copy.wait()


def filter_kernel(extent, field, pot, cy, cz, out, first_buf, second_buf):
    origin = REACH * DEGREE
    count = cy.shape[0] // field.shape[1]
    first_buf[...] = field[...]
    bufs = (first_buf, second_buf)
    for step in range(1, DEGREE + 1):
        src, other = bufs[(step - 1) % 2], bufs[step % 2]
        last = step == DEGREE
        margin = REACH * (DEGREE - step)
        prev = None if step == 1 else other
        dst, base = (out, 0) if last else (other, origin)

        def body(i, carry, src=src, dst=dst, base=base, prev=prev, margin=margin):
            at = i * count - margin
            planes = pot[pl.ds(origin + at, count)]
            apply_planes(src, origin + at, count, planes, cz, cy, dst, base + at, prev)
            return carry

        lax.fori_loop(0, (extent + 2 * margin) // count, body, 0)


def factor_kernel(
    n_gx, n_gy, cells, matrix, rfac, inverse, stack, ybuf, xbuf, ysend, yrecv, xsend, xrecv
):
    gx, gy = lax.axis_index("gx"), lax.axis_index("gy")
    norb = rfac.shape[0]
    nz = matrix.shape[1]
    lines = matrix.shape[0] // norb
    barrier = pltpu.get_barrier_semaphore()
    for k in range(1, n_gy):
        pl.semaphore_signal(
            barrier, inc=1, device_id=(gx, lax.rem(gy + k, n_gy)), device_id_type=MESH
        )
    for k in range(1, n_gx):
        pl.semaphore_signal(
            barrier, inc=1, device_id=(lax.rem(gx + k, n_gx), gy), device_id_type=MESH
        )

    for r in range(lines):
        for p, part in enumerate(split(matrix[pl.ds(r, norb, stride=lines)])):
            stack[p * norb : (p + 1) * norb, r * nz : (r + 1) * nz] = part
    square = lax.dot_general(
        stack[...], stack[...], (((1,), (1,)), ((), ())), preferred_element_type=jnp.float32
    )
    gram = None
    for p, q in ((2, 2), (1, 2), (2, 1), (0, 2), (2, 0), (1, 1), (0, 1), (1, 0), (0, 0)):
        term = square[p * norb : (p + 1) * norb, q * norb : (q + 1) * norb]
        gram = term if gram is None else gram + term
    pack = 128 // norb
    tall = norb // pack
    gram = gram / cells
    gram = jnp.concatenate([gram[i * tall : (i + 1) * tall] for i in range(pack)], axis=1)

    pl.semaphore_wait(barrier, n_gy + n_gx - 2)
    ybuf[gy] = gram
    copies = []
    for k in range(1, n_gy):
        copy = pltpu.make_async_remote_copy(
            ybuf.at[gy],
            ybuf.at[gy],
            ysend.at[k],
            yrecv.at[k],
            device_id=(gx, lax.rem(gy + k, n_gy)),
            device_id_type=MESH,
        )
        copy.start()
        copies.append(copy)
    for copy in copies:
        copy.wait()
    part = ybuf[0]
    for s in range(1, n_gy):
        part = part + ybuf[s]
    xbuf[gx] = part
    copies = []
    for k in range(1, n_gx):
        copy = pltpu.make_async_remote_copy(
            xbuf.at[gx],
            xbuf.at[gx],
            xsend.at[k],
            xrecv.at[k],
            device_id=(lax.rem(gx + k, n_gx), gy),
            device_id_type=MESH,
        )
        copy.start()
        copies.append(copy)
    for copy in copies:
        copy.wait()
    whole = xbuf[0]
    for s in range(1, n_gx):
        whole = whole + xbuf[s]

    row = lax.broadcasted_iota(jnp.int32, (norb, 128), 0)
    col = lax.broadcasted_iota(jnp.int32, (norb, 128), 1)
    whole = jnp.concatenate([whole[:, i * norb : (i + 1) * norb] for i in range(pack)], axis=0)
    whole = jnp.concatenate([whole, jnp.zeros((norb, 128 - norb), jnp.float32)], axis=1)
    table = jnp.where(col == row + norb, 1.0, whole)
    pivots = jnp.zeros((norb, 128), jnp.float32)
    for k in range(norb):
        pivot = table[k : k + 1, k : k + 1]
        pivots = jnp.where(row == k, pivot, pivots)
        ratio = jnp.where(row[:, :1] > k, table[:, k : k + 1] * (1.0 / pivot), 0.0)
        table = table - ratio * table[k : k + 1, :]
    table = table * lax.rsqrt(pivots)
    rfac[...] = jnp.where(row[:, :norb] <= col[:, :norb], table[:, :norb], 0.0)
    inverse[...] = table[:, norb : 2 * norb]


def mix_kernel(matrix, inverse, upper, out, rfac):
    rfac[...] = upper[...]
    norb = inverse.shape[0]
    lines = matrix.shape[0] // norb
    nz = matrix.shape[1]
    h, m, l = split(inverse[...])
    left = jnp.concatenate([h, h, h, m, m, l], axis=1)
    for r in range(0, lines, 2):
        both = jnp.concatenate(
            [matrix[pl.ds(r + i, norb, stride=lines)] for i in range(2)], axis=1
        )
        h, m, l = split(both)
        mixed = jnp.dot(
            left,
            jnp.concatenate([h, m, l, h, m, h], axis=0),
            preferred_element_type=jnp.float32,
        )
        for i in range(2):
            out[pl.ds(r + i, norb, stride=lines)] = mixed[:, i * nz : (i + 1) * nz]


def per_device(n_gx, n_gy, orbitals, potential):
    norb, bx, by, nz = orbitals.shape
    rows = norb // n_gy
    groups = n_gx // rows
    extent, ny = rows * bx, n_gy * by
    f32 = jnp.float32
    anywhere = pl.BlockSpec(memory_space=pltpu.HBM)
    vmem = pl.BlockSpec(memory_space=pltpu.VMEM)
    dma = pltpu.SemaphoreType.DMA
    gx_bits, gy_bits = rows.bit_length() - 1, n_gy.bit_length() - 1
    bits = gx_bits + gy_bits
    pot_shape = (2,) * gx_bits + (bx,) + (2,) * gy_bits + (by, nz)
    spread_sems = [dma((norb,)), dma((norb,)), dma((bits,)), dma((bits,)), dma((4,))]
    brick_shape = jax.ShapeDtypeStruct((norb, bx, by, nz), f32)

    yh, ym, yl = split_const(np.kron(np.eye(4), circulant(ny)))
    cy = jnp.asarray(np.concatenate([yh, yh, yh, ym, ym, yl], axis=1), f32)
    zh, zm, zl = split_const(circulant(nz))
    cz = jnp.asarray(np.concatenate([zh, zh, zh, zm, zm, zl], axis=0), f32)

    if groups == 1:
        planes = extent + 2 * REACH
        back = pl.pallas_call(
            functools.partial(whole_kernel, rows, n_gy),
            out_shape=brick_shape,
            in_specs=[anywhere] * 4,
            out_specs=vmem,
            scratch_shapes=[
                pltpu.VMEM(cy.shape, f32),
                pltpu.VMEM(cz.shape, f32),
                pltpu.VMEM(cy.shape, jnp.bfloat16),
                pltpu.VMEM(cz.shape, jnp.bfloat16),
                pltpu.VMEM((planes, ny, nz), f32),
                pltpu.VMEM((planes, ny, nz), f32),
                pltpu.VMEM(pot_shape, f32),
            ]
            + spread_sems
            + [dma((norb,)), dma((norb,))],
            compiler_params=pltpu.CompilerParams(
                collective_id=0, has_side_effects=True, vmem_limit_bytes=60 << 20
            ),
            name="spread_filter_return",
        )(orbitals, potential, cy, cz)
    else:
        field, allpot = pl.pallas_call(
            functools.partial(spread_kernel, rows, n_gy),
            out_shape=(
                jax.ShapeDtypeStruct((extent, ny, nz), f32),
                jax.ShapeDtypeStruct(pot_shape, f32),
            ),
            in_specs=[anywhere] * 2,
            out_specs=(anywhere, anywhere),
            scratch_shapes=spread_sems,
            compiler_params=pltpu.CompilerParams(collective_id=0, has_side_effects=True),
            name="spread",
        )(orbitals, potential)
        halo = REACH * DEGREE
        up = [(i, (i + rows) % n_gx) for i in range(n_gx)]
        down = [(t, s) for s, t in up]

        def widen(block):
            low = lax.ppermute(block[extent - halo :], "gx", up)
            high = lax.ppermute(block[:halo], "gx", down)
            return jnp.concatenate([low, block, high], axis=0)

        planes = extent + 2 * halo
        filtered = pl.pallas_call(
            functools.partial(filter_kernel, extent),
            out_shape=jax.ShapeDtypeStruct((extent, ny, nz), f32),
            in_specs=[vmem] * 4,
            out_specs=vmem,
            scratch_shapes=[pltpu.VMEM((planes, ny, nz), f32)] * 2,
            compiler_params=pltpu.CompilerParams(vmem_limit_bytes=24 << 20),
            name="filter",
        )(
            widen(field),
            widen(allpot.reshape(extent, ny, nz)),
            cy.astype(jnp.bfloat16),
            cz.astype(jnp.bfloat16),
        )
        back = pl.pallas_call(
            functools.partial(return_kernel, rows, n_gy),
            out_shape=brick_shape,
            in_specs=[anywhere],
            out_specs=anywhere,
            scratch_shapes=[dma((norb,)), dma((norb,)), dma],
            compiler_params=pltpu.CompilerParams(collective_id=1, has_side_effects=True),
            name="hand_back",
        )(filtered)

    matrix = back.reshape(norb * bx * by, nz)
    cells = float(bx * by * nz * n_gx * n_gy)
    upper, inverse = pl.pallas_call(
        functools.partial(factor_kernel, n_gx, n_gy, cells),
        out_shape=(jax.ShapeDtypeStruct((norb, norb), f32),) * 2,
        in_specs=[vmem],
        out_specs=(vmem, vmem),
        scratch_shapes=[
            pltpu.VMEM((3 * norb, bx * by * nz), jnp.bfloat16),
            pltpu.VMEM((n_gy, norb * norb // 128, 128), f32),
            pltpu.VMEM((n_gx, norb * norb // 128, 128), f32),
            dma((n_gy,)),
            dma((n_gy,)),
            dma((n_gx,)),
            dma((n_gx,)),
        ],
        compiler_params=pltpu.CompilerParams(
            collective_id=2, has_side_effects=True, vmem_limit_bytes=24 << 20
        ),
        name="factor",
    )(matrix)
    final, rfactor = pl.pallas_call(
        mix_kernel,
        out_shape=(
            jax.ShapeDtypeStruct(matrix.shape, f32),
            jax.ShapeDtypeStruct((norb, norb), f32),
        ),
        in_specs=[vmem] * 3,
        out_specs=(vmem, vmem),
        compiler_params=pltpu.CompilerParams(vmem_limit_bytes=24 << 20),
        name="mix",
    )(matrix, inverse, upper)
    return (final.reshape(orbitals.shape), rfactor)


def solution(mesh):
    return jax.shard_map(
        functools.partial(per_device, mesh.shape["gx"], mesh.shape["gy"]),
        mesh=mesh,
        in_specs=(P(None, "gx", "gy", None), P("gx", "gy", None)),
        out_specs=(P(None, "gx", "gy", None), P()),
        check_vma=False,
    )
```

```python
import functools
import numpy as np
import jax
import jax.numpy as jnp
from jax import lax
from jax.experimental import pallas as pl
from jax.experimental.pallas import tpu as pltpu
from jax.sharding import PartitionSpec as P

DEGREE = 3
REACH = 6
stencil_weights = (
    -5369.0 / 1800.0,
    12.0 / 7.0,
    -15.0 / 56.0,
    10.0 / 189.0,
    -1.0 / 112.0,
    2.0 / 1925.0,
    -1.0 / 16632.0,
)
grid_spacing = 0.5
filter_low = 4.0
filter_high = 46.0
centre_shift = 0.5 * (filter_high + filter_low)
half_width = 0.5 * (filter_high - filter_low)
scale = -0.5 / grid_spacing**2 / half_width
side_weights = tuple(scale * w for w in stencil_weights)
MESH = pl.DeviceIdType.MESH


def circulant(size):
    matrix = np.zeros((size, size), np.float64)
    for offset in range(1, REACH + 1):
        for i in range(size):
            matrix[i, (i + offset) % size] += side_weights[offset]
            matrix[i, (i - offset) % size] += side_weights[offset]
    return matrix


def split_const(matrix):
    parts, rest = [], matrix
    for _ in range(3):
        part = rest.astype(jnp.bfloat16)
        parts.append(part)
        rest = rest - part.astype(np.float64)
    return parts


def split(value):
    high = value.astype(jnp.bfloat16)
    rest = value - high.astype(jnp.float32)
    mid = rest.astype(jnp.bfloat16)
    low = (rest - mid.astype(jnp.float32)).astype(jnp.bfloat16)
    return high, mid, low


def place(rows):
    gx, gy = lax.axis_index("gx"), lax.axis_index("gy")
    inner = lax.rem(gx, rows)
    return gx - inner, inner, gy


def steps_far_near(rows, n_gy):
    steps = sorted(range(rows), key=lambda j: -min(j, rows - j))
    pairs = [(j, d) for j in steps for d in range(n_gy) if (j, d) != (0, 0)]
    mixed = []
    while pairs:
        mixed.append(pairs.pop(0))
        if pairs:
            mixed.append(pairs.pop())
    return mixed


def greet(rows, n_gy):
    first, inner, gy = place(rows)
    barrier = pltpu.get_barrier_semaphore()
    for j in range(rows):
        for d in range(n_gy):
            if (j, d) != (0, 0):
                who = (first + lax.rem(inner + j, rows), lax.rem(gy + d, n_gy))
                pl.semaphore_signal(barrier, inc=1, device_id=who, device_id_type=MESH)
    pl.semaphore_wait(barrier, rows * n_gy - 1)


def spread(
    rows, n_gy, origin, orb, pot, field, allpot, send, recv, psend, precv, own, meanwhile=None
):
    bx, by = pot.shape[0], pot.shape[1]
    first, inner, gy = place(rows)
    gx_bits, gy_bits = rows.bit_length() - 1, n_gy.bit_length() - 1
    bits = gx_bits + gy_bits
    member = inner * n_gy + gy
    mine = [lax.rem(member // (1 << (bits - 1 - b)), 2) for b in range(bits)]
    brick = field.at[
        pl.ds(origin + inner * bx, bx), pl.ds(pl.multiple_of(gy * by, by), by)
    ]

    def region(done):
        index = [slice(None) if b in done else mine[b] for b in range(bits)]
        return allpot.at[tuple(index[:gx_bits]) + (slice(None),) + tuple(index[gx_bits:])]

    def hop(stage, bit, done):
        t = member + (1 << (bits - 1 - bit)) * (1 - 2 * mine[bit])
        return pltpu.make_async_remote_copy(
            region(done),
            region(done),
            psend.at[stage],
            precv.at[stage],
            device_id=(first + t // n_gy, lax.rem(t, n_gy)),
            device_id_type=MESH,
        )

    plain = list(range(bits))
    swapped = list(plain)
    if bits >= 3:
        swapped[bits - 3], swapped[bits - 2] = bits - 2, bits - 3
    odd = mine[bits - 1] == 1

    def on_hop(stage, act):
        if plain[: stage + 1] == swapped[: stage + 1] or stage == bits - 1:
            act(hop(stage, plain[stage], plain[:stage]))
        else:
            pl.when(jnp.logical_not(odd))(
                lambda: act(hop(stage, plain[stage], plain[:stage]))
            )
            pl.when(odd)(lambda: act(hop(stage, swapped[stage], swapped[:stage])))

    keep = pltpu.make_async_copy(orb.at[member], brick, own.at[0])
    keep_pot = pltpu.make_async_copy(pot, region([]), own.at[1])
    keep.start()
    keep_pot.start()
    greet(rows, n_gy)
    keep_pot.wait()

    order = steps_far_near(rows, n_gy)
    copies = []
    per = -(-len(order) // max(bits, 1))
    for b in range(bits):
        on_hop(b, lambda copy: copy.start())
        for j, d in order[b * per : (b + 1) * per]:
            tx, ty = lax.rem(inner + j, rows), lax.rem(gy + d, n_gy)
            copy = pltpu.make_async_remote_copy(
                orb.at[tx * n_gy + ty],
                brick,
                send.at[j * n_gy + d],
                recv.at[j * n_gy + d],
                device_id=(first + tx, ty),
                device_id_type=MESH,
            )
            copy.start()
            copies.append(copy)
        on_hop(b, lambda copy: copy.wait())
    if meanwhile is not None:
        meanwhile()
    for copy in copies:
        copy.wait()
    keep.wait()


def send_block(rows, n_gy, origin, j, field, out, send, recv, own):
    bx, by = out.shape[1], out.shape[2]
    first, inner, gy = place(rows)
    member = inner * n_gy + gy
    tx = lax.rem(inner + j, rows)
    copies = []
    for d in range(n_gy):
        ty = lax.rem(gy + d, n_gy)
        part = field.at[
            pl.ds(origin + tx * bx, bx), pl.ds(pl.multiple_of(ty * by, by), by)
        ]
        if (j, d) == (0, 0):
            copy = pltpu.make_async_copy(part, out.at[member], own)
        else:
            copy = pltpu.make_async_remote_copy(
                part,
                out.at[member],
                send.at[j * n_gy + d],
                recv.at[j * n_gy + d],
                device_id=(first + tx, ty),
                device_id_type=MESH,
            )
        copy.start()
        copies.append(copy)
    return copies


def block_order(rows):
    steps = sorted(range(1, rows), key=lambda j: -min(j, rows - j))
    mixed = []
    while steps:
        mixed.append(steps.pop(0))
        if steps:
            mixed.append(steps.pop())
    return mixed + [0]


def apply_planes(src, here, count, pot_planes, cz, cy, dst, there, prev):
    ny, nz = src.shape[1], src.shape[2]
    half = cy.shape[1] // 2
    centre = src[pl.ds(here, count)]
    acc = ((pot_planes - centre_shift) * (1.0 / half_width) + 3.0 * side_weights[0]) * centre
    high, mid, low = split(centre.reshape(count * ny, nz))

    def dot(left, right):
        return jnp.dot(left, right, preferred_element_type=jnp.float32)

    def beside(value):
        return jnp.concatenate(
            [value[g : g + half] for g in range(0, count * ny, half)], axis=1
        )

    along = dot(jnp.concatenate([high, mid], axis=1), cz[:, : 2 * nz])
    lines = along[:, :nz] + along[:, nz:]
    lines = lines + dot(jnp.concatenate([low, high], axis=1), cz[:, 2 * nz :])
    high, mid, low = beside(high), beside(mid), beside(low)
    across = dot(cy[: 2 * half], jnp.concatenate([high, mid], axis=0))
    across = across[:half] + across[half:]
    across = across + dot(cy[2 * half :], jnp.concatenate([low, high], axis=0))
    lines = lines + jnp.concatenate(
        [across[:, g : g + nz] for g in range(0, across.shape[1], nz)], axis=0
    )
    for offset in range(1, REACH + 1):
        acc += side_weights[offset] * (
            src[pl.ds(here + offset, count)] + src[pl.ds(here - offset, count)]
        )
    acc += lines.reshape(count, ny, nz)
    if prev is not None:
        acc = 2.0 * acc - prev[pl.ds(here, count)]
    dst[pl.ds(there, count)] = acc


def whole_kernel(
    rows, n_gy, cells, orb, pot, cy_far, cz_far, out, rfac, inverse,
    back, stack, ybuf, xbuf, ysend, yrecv, xsend, xrecv,
    cy_wide, cz_wide, cy, cz, first_buf, second_buf, allpot, send, recv, psend, precv, own, bsend, brecv,
):
    bx, ny, nz = pot.shape[0], first_buf.shape[1], first_buf.shape[2]
    extent = rows * bx
    gx_bits = rows.bit_length() - 1
    fetch = [
        pltpu.make_async_copy(cy_far, cy_wide, own.at[2]),
        pltpu.make_async_copy(cz_far, cz_wide, own.at[3]),
    ]
    for copy in fetch:
        copy.start()

    def fetched():
        for copy in fetch:
            copy.wait()
        cy[...] = cy_wide[...].astype(jnp.bfloat16)
        cz[...] = cz_wide[...].astype(jnp.bfloat16)

    spread(rows, n_gy, REACH, orb, pot, first_buf, allpot, send, recv, psend, precv, own,
           fetched)
    _, inner, _ = place(rows)

    def pot_block(block):
        index = tuple(lax.rem(block // (1 << (gx_bits - 1 - b)), 2) for b in range(gx_bits))
        return allpot[index].reshape(bx, ny, nz)

    def wrap(buf):
        buf[0:REACH] = buf[extent : extent + REACH]
        buf[extent + REACH : extent + 2 * REACH] = buf[REACH : 2 * REACH]

    bufs = (first_buf, second_buf)
    copies = []
    for step in range(1, DEGREE + 1):
        src, other = bufs[(step - 1) % 2], bufs[step % 2]
        wrap(src)
        prev = None if step == 1 else other
        if step < DEGREE:

            def body(block, carry, src=src, other=other, prev=prev):
                at = REACH + block * bx
                apply_planes(src, at, bx, pot_block(block), cz, cy, other, at, prev)
                return carry

            lax.fori_loop(0, rows, body, 0, unroll=True)
        else:
            for j in block_order(rows):
                block = lax.rem(inner + j, rows)
                at = REACH + block * bx
                apply_planes(src, at, bx, pot_block(block), cz, cy, other, at, prev)
                copies += send_block(
                    rows, n_gy, REACH, j, other, back, bsend, brecv, own.at[0]
                )
    for copy in copies:
        copy.wait()
    keep = pltpu.make_async_copy(back, out, own.at[0])
    keep.start()
    flat = back.reshape(back.shape[0] * back.shape[1] * back.shape[2], nz)
    factor(
        rows, n_gy, cells, flat, rfac, inverse, stack, ybuf, xbuf, ysend, yrecv, xsend, xrecv
    )
    keep.wait()


def spread_kernel(rows, n_gy, orb, pot, field, allpot, send, recv, psend, precv, own):
    spread(rows, n_gy, 0, orb, pot, field, allpot, send, recv, psend, precv, own)


def return_kernel(rows, n_gy, field, out, send, recv, own):
    greet(rows, n_gy)
    copies = []
    for j in block_order(rows):
        copies += send_block(rows, n_gy, 0, j, field, out, send, recv, own)
    for copy in copies:
        copy.wait()


def filter_kernel(extent, field, pot, cy, cz, out, first_buf, second_buf):
    origin = REACH * DEGREE
    count = cy.shape[1] // 2 // field.shape[1]
    first_buf[...] = field[...]
    bufs = (first_buf, second_buf)
    for step in range(1, DEGREE + 1):
        src, other = bufs[(step - 1) % 2], bufs[step % 2]
        last = step == DEGREE
        margin = REACH * (DEGREE - step)
        prev = None if step == 1 else other
        dst, base = (out, 0) if last else (other, origin)

        def body(i, carry, src=src, dst=dst, base=base, prev=prev, margin=margin):
            at = i * count - margin
            planes = pot[pl.ds(origin + at, count)]
            apply_planes(src, origin + at, count, planes, cz, cy, dst, base + at, prev)
            return carry

        lax.fori_loop(0, (extent + 2 * margin) // count, body, 0)


def greet_lines(n_gx, n_gy):
    gx, gy = lax.axis_index("gx"), lax.axis_index("gy")
    barrier = pltpu.get_barrier_semaphore()
    for k in range(1, n_gy):
        pl.semaphore_signal(
            barrier, inc=1, device_id=(gx, lax.rem(gy + k, n_gy)), device_id_type=MESH
        )
    for k in range(1, n_gx):
        pl.semaphore_signal(
            barrier, inc=1, device_id=(lax.rem(gx + k, n_gx), gy), device_id_type=MESH
        )
    pl.semaphore_wait(barrier, n_gy + n_gx - 2)


def factor_kernel(n_gx, n_gy, cells, *refs):
    greet_lines(n_gx, n_gy)
    factor(n_gx, n_gy, cells, *refs)


def factor(
    n_gx, n_gy, cells, matrix, rfac, inverse, stack, ybuf, xbuf, ysend, yrecv, xsend, xrecv
):
    gx, gy = lax.axis_index("gx"), lax.axis_index("gy")
    norb = rfac.shape[0]
    nz = matrix.shape[1]
    lines = matrix.shape[0] // norb
    for r in range(lines):
        for p, part in enumerate(split(matrix[pl.ds(r, norb, stride=lines)])):
            stack[p * norb : (p + 1) * norb, r * nz : (r + 1) * nz] = part
    square = lax.dot_general(
        stack[...], stack[...], (((1,), (1,)), ((), ())), preferred_element_type=jnp.float32
    )
    gram = None
    for p, q in ((2, 2), (1, 2), (2, 1), (0, 2), (2, 0), (1, 1), (0, 1), (1, 0), (0, 0)):
        term = square[p * norb : (p + 1) * norb, q * norb : (q + 1) * norb]
        gram = term if gram is None else gram + term
    pack = 128 // norb
    tall = norb // pack
    gram = gram / cells
    gram = jnp.concatenate([gram[i * tall : (i + 1) * tall] for i in range(pack)], axis=1)

    ybuf[gy] = gram
    copies = []
    for k in range(1, n_gy):
        copy = pltpu.make_async_remote_copy(
            ybuf.at[gy],
            ybuf.at[gy],
            ysend.at[k],
            yrecv.at[k],
            device_id=(gx, lax.rem(gy + k, n_gy)),
            device_id_type=MESH,
        )
        copy.start()
        copies.append(copy)
    for copy in copies:
        copy.wait()
    part = ybuf[0]
    for s in range(1, n_gy):
        part = part + ybuf[s]
    xbuf[gx] = part
    copies = []
    for k in range(1, n_gx):
        copy = pltpu.make_async_remote_copy(
            xbuf.at[gx],
            xbuf.at[gx],
            xsend.at[k],
            xrecv.at[k],
            device_id=(lax.rem(gx + k, n_gx), gy),
            device_id_type=MESH,
        )
        copy.start()
        copies.append(copy)
    for copy in copies:
        copy.wait()
    whole = xbuf[0]
    for s in range(1, n_gx):
        whole = whole + xbuf[s]

    row = lax.broadcasted_iota(jnp.int32, (norb, 128), 0)
    col = lax.broadcasted_iota(jnp.int32, (norb, 128), 1)
    whole = jnp.concatenate([whole[:, i * norb : (i + 1) * norb] for i in range(pack)], axis=0)
    whole = jnp.concatenate([whole, jnp.zeros((norb, 128 - norb), jnp.float32)], axis=1)
    table = jnp.where(col == row + norb, 1.0, whole)
    pivots = jnp.zeros((norb, 128), jnp.float32)
    for k in range(norb):
        pivot = table[k : k + 1, k : k + 1]
        pivots = jnp.where(row == k, pivot, pivots)
        ratio = jnp.where(row[:, :1] > k, table[:, k : k + 1] * (1.0 / pivot), 0.0)
        table = table - ratio * table[k : k + 1, :]
    table = table * lax.rsqrt(pivots)
    rfac[...] = jnp.where(row[:, :norb] <= col[:, :norb], table[:, :norb], 0.0)
    inverse[...] = table[:, norb : 2 * norb]


def mix_kernel(bricks, inverse, upper, out, rfac):
    norb, lines, nz = bricks.shape
    rfac[...] = upper[...]
    matrix, mixed_rows = bricks.reshape(norb * lines, nz), out.reshape(norb * lines, nz)
    h, m, l = split(inverse[...])
    left = jnp.concatenate([h, h, h, m, m, l], axis=1)
    for r in range(0, lines, 2):
        both = jnp.concatenate(
            [matrix[pl.ds(r + i, norb, stride=lines)] for i in range(2)], axis=1
        )
        h, m, l = split(both)
        mixed = jnp.dot(
            left,
            jnp.concatenate([h, m, l, h, m, h], axis=0),
            preferred_element_type=jnp.float32,
        )
        for i in range(2):
            mixed_rows[pl.ds(r + i, norb, stride=lines)] = mixed[:, i * nz : (i + 1) * nz]


def per_device(n_gx, n_gy, orbitals, potential):
    norb, bx, by, nz = orbitals.shape
    rows = norb // n_gy
    groups = n_gx // rows
    extent, ny = rows * bx, n_gy * by
    f32 = jnp.float32
    anywhere = pl.BlockSpec(memory_space=pltpu.HBM)
    vmem = pl.BlockSpec(memory_space=pltpu.VMEM)
    dma = pltpu.SemaphoreType.DMA
    gx_bits, gy_bits = rows.bit_length() - 1, n_gy.bit_length() - 1
    bits = gx_bits + gy_bits
    pot_shape = (2,) * gx_bits + (bx,) + (2,) * gy_bits + (by, nz)
    spread_sems = [dma((norb,)), dma((norb,)), dma((bits,)), dma((bits,)), dma((4,))]
    brick_shape = jax.ShapeDtypeStruct((norb, bx, by, nz), f32)

    yh, ym, yl = split_const(np.kron(np.eye(4), circulant(ny)))
    cy = jnp.asarray(np.block([[yh, yh], [ym, ym], [yh, yl]]), f32)
    zh, zm, zl = split_const(circulant(nz))
    cz = jnp.asarray(np.block([[zh, zm, zh], [zh, zm, zl]]), f32)

    cells = float(bx * by * nz * n_gx * n_gy)
    small = (jax.ShapeDtypeStruct((norb, norb), f32),) * 2
    factor_scratch = [
        pltpu.VMEM((3 * norb, bx * by * nz), jnp.bfloat16),
        pltpu.VMEM((n_gy, norb * norb // 128, 128), f32),
        pltpu.VMEM((n_gx, norb * norb // 128, 128), f32),
        dma((n_gy,)),
        dma((n_gy,)),
        dma((n_gx,)),
        dma((n_gx,)),
    ]

    if groups == 1:
        planes = extent + 2 * REACH
        back, upper, inverse = pl.pallas_call(
            functools.partial(whole_kernel, rows, n_gy, cells),
            out_shape=(brick_shape,) + small,
            in_specs=[anywhere] * 4,
            out_specs=(anywhere, vmem, vmem),
            scratch_shapes=[pltpu.VMEM(brick_shape.shape, f32)]
            + factor_scratch
            + [
                pltpu.VMEM(cy.shape, f32),
                pltpu.VMEM(cz.shape, f32),
                pltpu.VMEM(cy.shape, jnp.bfloat16),
                pltpu.VMEM(cz.shape, jnp.bfloat16),
                pltpu.VMEM((planes, ny, nz), f32),
                pltpu.VMEM((planes, ny, nz), f32),
                pltpu.VMEM(pot_shape, f32),
            ]
            + spread_sems
            + [dma((norb,)), dma((norb,))],
            compiler_params=pltpu.CompilerParams(
                collective_id=0, has_side_effects=True, vmem_limit_bytes=60 << 20
            ),
            name="spread_filter_return_factor",
        )(orbitals, potential, cy, cz)
    else:
        field, allpot = pl.pallas_call(
            functools.partial(spread_kernel, rows, n_gy),
            out_shape=(
                jax.ShapeDtypeStruct((extent, ny, nz), f32),
                jax.ShapeDtypeStruct(pot_shape, f32),
            ),
            in_specs=[anywhere] * 2,
            out_specs=(anywhere, anywhere),
            scratch_shapes=spread_sems,
            compiler_params=pltpu.CompilerParams(collective_id=0, has_side_effects=True),
            name="spread",
        )(orbitals, potential)
        halo = REACH * DEGREE
        up = [(i, (i + rows) % n_gx) for i in range(n_gx)]
        down = [(t, s) for s, t in up]

        def widen(block):
            low = lax.ppermute(block[extent - halo :], "gx", up)
            high = lax.ppermute(block[:halo], "gx", down)
            return jnp.concatenate([low, block, high], axis=0)

        planes = extent + 2 * halo
        filtered = pl.pallas_call(
            functools.partial(filter_kernel, extent),
            out_shape=jax.ShapeDtypeStruct((extent, ny, nz), f32),
            in_specs=[vmem] * 4,
            out_specs=vmem,
            scratch_shapes=[pltpu.VMEM((planes, ny, nz), f32)] * 2,
            compiler_params=pltpu.CompilerParams(vmem_limit_bytes=24 << 20),
            name="filter",
        )(
            widen(field),
            widen(allpot.reshape(extent, ny, nz)),
            cy.astype(jnp.bfloat16),
            cz.astype(jnp.bfloat16),
        )
        back = pl.pallas_call(
            functools.partial(return_kernel, rows, n_gy),
            out_shape=brick_shape,
            in_specs=[anywhere],
            out_specs=anywhere,
            scratch_shapes=[dma((norb,)), dma((norb,)), dma],
            compiler_params=pltpu.CompilerParams(collective_id=1, has_side_effects=True),
            name="hand_back",
        )(filtered)

        upper, inverse = pl.pallas_call(
            functools.partial(factor_kernel, n_gx, n_gy, cells),
            out_shape=small,
            in_specs=[vmem],
            out_specs=(vmem, vmem),
            scratch_shapes=factor_scratch,
            compiler_params=pltpu.CompilerParams(
                collective_id=2, has_side_effects=True, vmem_limit_bytes=24 << 20
            ),
            name="factor",
        )(back.reshape(norb * bx * by, nz))

    piece = 2 * by
    block = pl.BlockSpec((norb, piece, nz), lambda i: (0, i, 0))
    square = pl.BlockSpec((norb, norb), lambda i: (0, 0))
    final, rfactor = pl.pallas_call(
        mix_kernel,
        grid=(bx * by // piece,),
        out_shape=(jax.ShapeDtypeStruct((norb, bx * by, nz), f32), small[0]),
        in_specs=[block, square, square],
        out_specs=(block, square),
        compiler_params=pltpu.CompilerParams(vmem_limit_bytes=60 << 20),
        name="mix",
    )(back.reshape(norb, bx * by, nz), inverse, upper)
    return (final.reshape(orbitals.shape), rfactor)


def solution(mesh):
    return jax.shard_map(
        functools.partial(per_device, mesh.shape["gx"], mesh.shape["gy"]),
        mesh=mesh,
        in_specs=(P(None, "gx", "gy", None), P("gx", "gy", None)),
        out_specs=(P(None, "gx", "gy", None), P()),
        check_vma=False,
    )
```

```python
import functools
import numpy as np
import jax
import jax.numpy as jnp
from jax import lax
from jax.experimental import pallas as pl
from jax.experimental.pallas import tpu as pltpu
from jax.sharding import PartitionSpec as P

DEGREE = 3
REACH = 6
stencil_weights = (
    -5369.0 / 1800.0,
    12.0 / 7.0,
    -15.0 / 56.0,
    10.0 / 189.0,
    -1.0 / 112.0,
    2.0 / 1925.0,
    -1.0 / 16632.0,
)
grid_spacing = 0.5
filter_low = 4.0
filter_high = 46.0
centre_shift = 0.5 * (filter_high + filter_low)
half_width = 0.5 * (filter_high - filter_low)
scale = -0.5 / grid_spacing**2 / half_width
side_weights = tuple(scale * w for w in stencil_weights)
MESH = pl.DeviceIdType.MESH


def circulant(size):
    matrix = np.zeros((size, size), np.float64)
    for offset in range(1, REACH + 1):
        for i in range(size):
            matrix[i, (i + offset) % size] += side_weights[offset]
            matrix[i, (i - offset) % size] += side_weights[offset]
    return matrix


def split_const(matrix):
    parts, rest = [], matrix
    for _ in range(3):
        part = rest.astype(jnp.bfloat16)
        parts.append(part)
        rest = rest - part.astype(np.float64)
    return parts


def split(value):
    high = value.astype(jnp.bfloat16)
    rest = value - high.astype(jnp.float32)
    mid = rest.astype(jnp.bfloat16)
    low = (rest - mid.astype(jnp.float32)).astype(jnp.bfloat16)
    return high, mid, low


def place(rows):
    gx, gy = lax.axis_index("gx"), lax.axis_index("gy")
    inner = lax.rem(gx, rows)
    return gx - inner, inner, gy


def steps_far_near(rows, n_gy):
    steps = sorted(range(rows), key=lambda j: -min(j, rows - j))
    pairs = [(j, d) for j in steps for d in range(n_gy) if (j, d) != (0, 0)]
    mixed = []
    while pairs:
        mixed.append(pairs.pop(0))
        if pairs:
            mixed.append(pairs.pop())
    return mixed


def greet(rows, n_gy):
    first, inner, gy = place(rows)
    barrier = pltpu.get_barrier_semaphore()
    for j in range(rows):
        for d in range(n_gy):
            if (j, d) != (0, 0):
                who = (first + lax.rem(inner + j, rows), lax.rem(gy + d, n_gy))
                pl.semaphore_signal(barrier, inc=1, device_id=who, device_id_type=MESH)
    pl.semaphore_wait(barrier, rows * n_gy - 1)


def spread(
    rows, n_gy, origin, orb, pot, field, allpot, send, recv, psend, precv, own, meanwhile=None
):
    bx, by = pot.shape[0], pot.shape[1]
    first, inner, gy = place(rows)
    gx_bits, gy_bits = rows.bit_length() - 1, n_gy.bit_length() - 1
    bits = gx_bits + gy_bits
    member = inner * n_gy + gy
    mine = [lax.rem(member // (1 << (bits - 1 - b)), 2) for b in range(bits)]
    brick = field.at[
        pl.ds(origin + inner * bx, bx), pl.ds(pl.multiple_of(gy * by, by), by)
    ]

    def region(done):
        index = [slice(None) if b in done else mine[b] for b in range(bits)]
        return allpot.at[tuple(index[:gx_bits]) + (slice(None),) + tuple(index[gx_bits:])]

    def hop(stage, bit, done):
        t = member + (1 << (bits - 1 - bit)) * (1 - 2 * mine[bit])
        return pltpu.make_async_remote_copy(
            region(done),
            region(done),
            psend.at[stage],
            precv.at[stage],
            device_id=(first + t // n_gy, lax.rem(t, n_gy)),
            device_id_type=MESH,
        )

    plain = list(range(bits))
    swapped = list(plain)
    if bits >= 3:
        swapped[bits - 3], swapped[bits - 2] = bits - 2, bits - 3
    odd = mine[bits - 1] == 1

    def on_hop(stage, act):
        if plain[: stage + 1] == swapped[: stage + 1] or stage == bits - 1:
            act(hop(stage, plain[stage], plain[:stage]))
        else:
            pl.when(jnp.logical_not(odd))(
                lambda: act(hop(stage, plain[stage], plain[:stage]))
            )
            pl.when(odd)(lambda: act(hop(stage, swapped[stage], swapped[:stage])))

    keep = pltpu.make_async_copy(orb.at[member], brick, own.at[0])
    keep_pot = pltpu.make_async_copy(pot, region([]), own.at[1])
    keep.start()
    keep_pot.start()
    greet(rows, n_gy)
    keep_pot.wait()

    order = steps_far_near(rows, n_gy)
    copies = []
    per = len(order) // (bits + 2)
    cuts = [per * b for b in range(bits)] + [len(order)]
    for b in range(bits):
        on_hop(b, lambda copy: copy.start())
        for j, d in order[cuts[b] : cuts[b + 1]]:
            tx, ty = lax.rem(inner + j, rows), lax.rem(gy + d, n_gy)
            copy = pltpu.make_async_remote_copy(
                orb.at[tx * n_gy + ty],
                brick,
                send.at[j * n_gy + d],
                recv.at[j * n_gy + d],
                device_id=(first + tx, ty),
                device_id_type=MESH,
            )
            copy.start()
            copies.append(copy)
        on_hop(b, lambda copy: copy.wait())
    if meanwhile is not None:
        meanwhile()
    for copy in copies:
        copy.wait()
    keep.wait()


def send_block(rows, n_gy, origin, j, field, out, send, recv, own):
    bx, by = out.shape[1], out.shape[2]
    first, inner, gy = place(rows)
    member = inner * n_gy + gy
    tx = lax.rem(inner + j, rows)
    copies = []
    for d in range(n_gy):
        ty = lax.rem(gy + d, n_gy)
        part = field.at[
            pl.ds(origin + tx * bx, bx), pl.ds(pl.multiple_of(ty * by, by), by)
        ]
        if (j, d) == (0, 0):
            copy = pltpu.make_async_copy(part, out.at[member], own)
        else:
            copy = pltpu.make_async_remote_copy(
                part,
                out.at[member],
                send.at[j * n_gy + d],
                recv.at[j * n_gy + d],
                device_id=(first + tx, ty),
                device_id_type=MESH,
            )
        copy.start()
        copies.append(copy)
    return copies


def block_order(rows):
    steps = sorted(range(1, rows), key=lambda j: -min(j, rows - j))
    mixed = []
    while steps:
        mixed.append(steps.pop(0))
        if steps:
            mixed.append(steps.pop())
    return mixed + [0]


def apply_planes(src, here, count, pot_planes, cz, cy, dst, there, prev):
    ny, nz = src.shape[1], src.shape[2]
    half = cy.shape[1] // 2
    centre = src[pl.ds(here, count)]
    acc = ((pot_planes - centre_shift) * (1.0 / half_width) + 3.0 * side_weights[0]) * centre
    high, mid, low = split(centre.reshape(count * ny, nz))

    def dot(left, right):
        return jnp.dot(left, right, preferred_element_type=jnp.float32)

    def beside(value):
        return jnp.concatenate(
            [value[g : g + half] for g in range(0, count * ny, half)], axis=1
        )

    along = dot(jnp.concatenate([high, mid], axis=1), cz[:, : 2 * nz])
    lines = along[:, :nz] + along[:, nz:]
    lines = lines + dot(jnp.concatenate([low, high], axis=1), cz[:, 2 * nz :])
    high, mid, low = beside(high), beside(mid), beside(low)
    across = dot(cy[: 2 * half], jnp.concatenate([high, mid], axis=0))
    across = across[:half] + across[half:]
    across = across + dot(cy[2 * half :], jnp.concatenate([low, high], axis=0))
    lines = lines + jnp.concatenate(
        [across[:, g : g + nz] for g in range(0, across.shape[1], nz)], axis=0
    )
    for offset in range(1, REACH + 1):
        acc += side_weights[offset] * (
            src[pl.ds(here + offset, count)] + src[pl.ds(here - offset, count)]
        )
    acc += lines.reshape(count, ny, nz)
    if prev is not None:
        acc = 2.0 * acc - prev[pl.ds(here, count)]
    dst[pl.ds(there, count)] = acc


def whole_kernel(
    rows, n_gy, cells, orb, pot, cy_far, cz_far, out, rfac,
    inverse, back, stack, ybuf, xbuf, ysend, yrecv, xsend, xrecv,
    cy_wide, cz_wide, cy, cz, first_buf, second_buf, allpot, send, recv, psend, precv, own, bsend, brecv,
):
    bx, ny, nz = pot.shape[0], first_buf.shape[1], first_buf.shape[2]
    extent = rows * bx
    gx_bits = rows.bit_length() - 1
    fetch = [
        pltpu.make_async_copy(cy_far, cy_wide, own.at[2]),
        pltpu.make_async_copy(cz_far, cz_wide, own.at[3]),
    ]
    for copy in fetch:
        copy.start()

    def fetched():
        for copy in fetch:
            copy.wait()
        cy[...] = cy_wide[...].astype(jnp.bfloat16)
        cz[...] = cz_wide[...].astype(jnp.bfloat16)

    spread(rows, n_gy, REACH, orb, pot, first_buf, allpot, send, recv, psend, precv, own,
           fetched)
    _, inner, _ = place(rows)

    def pot_block(block):
        index = tuple(lax.rem(block // (1 << (gx_bits - 1 - b)), 2) for b in range(gx_bits))
        return allpot[index].reshape(bx, ny, nz)

    def wrap(buf):
        buf[0:REACH] = buf[extent : extent + REACH]
        buf[extent + REACH : extent + 2 * REACH] = buf[REACH : 2 * REACH]

    bufs = (first_buf, second_buf)
    copies = []
    for step in range(1, DEGREE + 1):
        src, other = bufs[(step - 1) % 2], bufs[step % 2]
        wrap(src)
        prev = None if step == 1 else other
        if step < DEGREE:

            def body(block, carry, src=src, other=other, prev=prev):
                at = REACH + block * bx
                apply_planes(src, at, bx, pot_block(block), cz, cy, other, at, prev)
                return carry

            lax.fori_loop(0, rows, body, 0, unroll=True)
        else:
            for j in block_order(rows):
                block = lax.rem(inner + j, rows)
                at = REACH + block * bx
                apply_planes(src, at, bx, pot_block(block), cz, cy, other, at, prev)
                copies += send_block(
                    rows, n_gy, REACH, j, other, back, bsend, brecv, own.at[0]
                )
    for copy in copies:
        copy.wait()
    flat = back.reshape(back.shape[0] * back.shape[1] * back.shape[2], nz)
    factor(
        rows, n_gy, cells, flat, rfac, inverse, stack, ybuf, xbuf, ysend, yrecv, xsend, xrecv
    )
    mix(flat, inverse, out.reshape(flat.shape))


def spread_kernel(rows, n_gy, orb, pot, field, allpot, send, recv, psend, precv, own):
    spread(rows, n_gy, 0, orb, pot, field, allpot, send, recv, psend, precv, own)


def return_kernel(rows, n_gy, field, out, send, recv, own):
    greet(rows, n_gy)
    copies = []
    for j in block_order(rows):
        copies += send_block(rows, n_gy, 0, j, field, out, send, recv, own)
    for copy in copies:
        copy.wait()


def filter_kernel(extent, field, pot, cy, cz, out, first_buf, second_buf):
    origin = REACH * DEGREE
    count = cy.shape[1] // 2 // field.shape[1]
    first_buf[...] = field[...]
    bufs = (first_buf, second_buf)
    for step in range(1, DEGREE + 1):
        src, other = bufs[(step - 1) % 2], bufs[step % 2]
        last = step == DEGREE
        margin = REACH * (DEGREE - step)
        prev = None if step == 1 else other
        dst, base = (out, 0) if last else (other, origin)

        def body(i, carry, src=src, dst=dst, base=base, prev=prev, margin=margin):
            at = i * count - margin
            planes = pot[pl.ds(origin + at, count)]
            apply_planes(src, origin + at, count, planes, cz, cy, dst, base + at, prev)
            return carry

        lax.fori_loop(0, (extent + 2 * margin) // count, body, 0)


def greet_lines(n_gx, n_gy):
    gx, gy = lax.axis_index("gx"), lax.axis_index("gy")
    barrier = pltpu.get_barrier_semaphore()
    for k in range(1, n_gy):
        pl.semaphore_signal(
            barrier, inc=1, device_id=(gx, lax.rem(gy + k, n_gy)), device_id_type=MESH
        )
    for k in range(1, n_gx):
        pl.semaphore_signal(
            barrier, inc=1, device_id=(lax.rem(gx + k, n_gx), gy), device_id_type=MESH
        )
    pl.semaphore_wait(barrier, n_gy + n_gx - 2)


def factor_kernel(n_gx, n_gy, cells, *refs):
    greet_lines(n_gx, n_gy)
    factor(n_gx, n_gy, cells, *refs)


def factor(
    n_gx, n_gy, cells, matrix, rfac, inverse, stack, ybuf, xbuf, ysend, yrecv, xsend, xrecv
):
    gx, gy = lax.axis_index("gx"), lax.axis_index("gy")
    norb = rfac.shape[0]
    nz = matrix.shape[1]
    lines = matrix.shape[0] // norb
    for r in range(lines):
        for p, part in enumerate(split(matrix[pl.ds(r, norb, stride=lines)])):
            stack[p * norb : (p + 1) * norb, r * nz : (r + 1) * nz] = part
    square = lax.dot_general(
        stack[...], stack[...], (((1,), (1,)), ((), ())), preferred_element_type=jnp.float32
    )
    gram = None
    for p, q in ((2, 2), (1, 2), (2, 1), (0, 2), (2, 0), (1, 1), (0, 1), (1, 0), (0, 0)):
        term = square[p * norb : (p + 1) * norb, q * norb : (q + 1) * norb]
        gram = term if gram is None else gram + term
    pack = 128 // norb
    tall = norb // pack
    gram = gram / cells
    gram = jnp.concatenate([gram[i * tall : (i + 1) * tall] for i in range(pack)], axis=1)

    ybuf[gy] = gram
    copies = []
    for k in range(1, n_gy):
        copy = pltpu.make_async_remote_copy(
            ybuf.at[gy],
            ybuf.at[gy],
            ysend.at[k],
            yrecv.at[k],
            device_id=(gx, lax.rem(gy + k, n_gy)),
            device_id_type=MESH,
        )
        copy.start()
        copies.append(copy)
    for copy in copies:
        copy.wait()
    part = ybuf[0]
    for s in range(1, n_gy):
        part = part + ybuf[s]
    xbuf[gx] = part
    copies = []
    for k in range(1, n_gx):
        copy = pltpu.make_async_remote_copy(
            xbuf.at[gx],
            xbuf.at[gx],
            xsend.at[k],
            xrecv.at[k],
            device_id=(lax.rem(gx + k, n_gx), gy),
            device_id_type=MESH,
        )
        copy.start()
        copies.append(copy)
    for copy in copies:
        copy.wait()
    whole = xbuf[0]
    for s in range(1, n_gx):
        whole = whole + xbuf[s]

    row = lax.broadcasted_iota(jnp.int32, (norb, 128), 0)
    col = lax.broadcasted_iota(jnp.int32, (norb, 128), 1)
    whole = jnp.concatenate([whole[:, i * norb : (i + 1) * norb] for i in range(pack)], axis=0)
    whole = jnp.concatenate([whole, jnp.zeros((norb, 128 - norb), jnp.float32)], axis=1)
    table = jnp.where(col == row + norb, 1.0, whole)
    pivots = jnp.zeros((norb, 128), jnp.float32)
    for k in range(norb):
        pivot = table[k : k + 1, k : k + 1]
        pivots = jnp.where(row == k, pivot, pivots)
        ratio = jnp.where(row[:, :1] > k, table[:, k : k + 1] * (1.0 / pivot), 0.0)
        table = table - ratio * table[k : k + 1, :]
    table = table * lax.rsqrt(pivots)
    rfac[...] = jnp.where(row[:, :norb] <= col[:, :norb], table[:, :norb], 0.0)
    inverse[...] = table[:, norb : 2 * norb]


def mix_kernel(bricks, inverse, upper, out, rfac):
    norb, lines, nz = bricks.shape
    rfac[...] = upper[...]
    mix(bricks.reshape(norb * lines, nz), inverse, out.reshape(norb * lines, nz))


def mix(matrix, inverse, mixed_rows):
    norb = inverse.shape[0]
    lines, nz = matrix.shape[0] // norb, matrix.shape[1]
    h, m, l = split(inverse[...])
    left = jnp.concatenate([h, h, h, m, m, l], axis=1)
    for r in range(0, lines, 2):
        both = jnp.concatenate(
            [matrix[pl.ds(r + i, norb, stride=lines)] for i in range(2)], axis=1
        )
        h, m, l = split(both)
        mixed = jnp.dot(
            left,
            jnp.concatenate([h, m, l, h, m, h], axis=0),
            preferred_element_type=jnp.float32,
        )
        for i in range(2):
            mixed_rows[pl.ds(r + i, norb, stride=lines)] = mixed[:, i * nz : (i + 1) * nz]


def per_device(n_gx, n_gy, orbitals, potential):
    norb, bx, by, nz = orbitals.shape
    rows = norb // n_gy
    groups = n_gx // rows
    extent, ny = rows * bx, n_gy * by
    f32 = jnp.float32
    anywhere = pl.BlockSpec(memory_space=pltpu.HBM)
    vmem = pl.BlockSpec(memory_space=pltpu.VMEM)
    dma = pltpu.SemaphoreType.DMA
    gx_bits, gy_bits = rows.bit_length() - 1, n_gy.bit_length() - 1
    bits = gx_bits + gy_bits
    pot_shape = (2,) * gx_bits + (bx,) + (2,) * gy_bits + (by, nz)
    spread_sems = [dma((norb,)), dma((norb,)), dma((bits,)), dma((bits,)), dma((4,))]
    brick_shape = jax.ShapeDtypeStruct((norb, bx, by, nz), f32)

    yh, ym, yl = split_const(np.kron(np.eye(4), circulant(ny)))
    cy = jnp.asarray(np.block([[yh, yh], [ym, ym], [yh, yl]]), f32)
    zh, zm, zl = split_const(circulant(nz))
    cz = jnp.asarray(np.block([[zh, zm, zh], [zh, zm, zl]]), f32)

    cells = float(bx * by * nz * n_gx * n_gy)
    small = (jax.ShapeDtypeStruct((norb, norb), f32),) * 2
    factor_scratch = [
        pltpu.VMEM((3 * norb, bx * by * nz), jnp.bfloat16),
        pltpu.VMEM((n_gy, norb * norb // 128, 128), f32),
        pltpu.VMEM((n_gx, norb * norb // 128, 128), f32),
        dma((n_gy,)),
        dma((n_gy,)),
        dma((n_gx,)),
        dma((n_gx,)),
    ]

    if groups == 1:
        planes = extent + 2 * REACH
        return pl.pallas_call(
            functools.partial(whole_kernel, rows, n_gy, cells),
            out_shape=(brick_shape, small[0]),
            in_specs=[anywhere] * 4,
            out_specs=(vmem, vmem),
            scratch_shapes=[pltpu.VMEM((norb, norb), f32), pltpu.VMEM(brick_shape.shape, f32)]
            + factor_scratch
            + [
                pltpu.VMEM(cy.shape, f32),
                pltpu.VMEM(cz.shape, f32),
                pltpu.VMEM(cy.shape, jnp.bfloat16),
                pltpu.VMEM(cz.shape, jnp.bfloat16),
                pltpu.VMEM((planes, ny, nz), f32),
                pltpu.VMEM((planes, ny, nz), f32),
                pltpu.VMEM(pot_shape, f32),
            ]
            + spread_sems
            + [dma((norb,)), dma((norb,))],
            compiler_params=pltpu.CompilerParams(
                collective_id=0, has_side_effects=True, vmem_limit_bytes=60 << 20
            ),
            name="whole_step",
        )(orbitals, potential, cy, cz)
    else:
        field, allpot = pl.pallas_call(
            functools.partial(spread_kernel, rows, n_gy),
            out_shape=(
                jax.ShapeDtypeStruct((extent, ny, nz), f32),
                jax.ShapeDtypeStruct(pot_shape, f32),
            ),
            in_specs=[anywhere] * 2,
            out_specs=(anywhere, anywhere),
            scratch_shapes=spread_sems,
            compiler_params=pltpu.CompilerParams(collective_id=0, has_side_effects=True),
            name="spread",
        )(orbitals, potential)
        halo = REACH * DEGREE
        up = [(i, (i + rows) % n_gx) for i in range(n_gx)]
        down = [(t, s) for s, t in up]

        def widen(block):
            low = lax.ppermute(block[extent - halo :], "gx", up)
            high = lax.ppermute(block[:halo], "gx", down)
            return jnp.concatenate([low, block, high], axis=0)

        planes = extent + 2 * halo
        filtered = pl.pallas_call(
            functools.partial(filter_kernel, extent),
            out_shape=jax.ShapeDtypeStruct((extent, ny, nz), f32),
            in_specs=[vmem] * 4,
            out_specs=vmem,
            scratch_shapes=[pltpu.VMEM((planes, ny, nz), f32)] * 2,
            compiler_params=pltpu.CompilerParams(vmem_limit_bytes=24 << 20),
            name="filter",
        )(
            widen(field),
            widen(allpot.reshape(extent, ny, nz)),
            cy.astype(jnp.bfloat16),
            cz.astype(jnp.bfloat16),
        )
        back = pl.pallas_call(
            functools.partial(return_kernel, rows, n_gy),
            out_shape=brick_shape,
            in_specs=[anywhere],
            out_specs=anywhere,
            scratch_shapes=[dma((norb,)), dma((norb,)), dma],
            compiler_params=pltpu.CompilerParams(collective_id=1, has_side_effects=True),
            name="hand_back",
        )(filtered)

        upper, inverse = pl.pallas_call(
            functools.partial(factor_kernel, n_gx, n_gy, cells),
            out_shape=small,
            in_specs=[vmem],
            out_specs=(vmem, vmem),
            scratch_shapes=factor_scratch,
            compiler_params=pltpu.CompilerParams(
                collective_id=2, has_side_effects=True, vmem_limit_bytes=24 << 20
            ),
            name="factor",
        )(back.reshape(norb * bx * by, nz))

    piece = 2 * by
    block = pl.BlockSpec((norb, piece, nz), lambda i: (0, i, 0))
    square = pl.BlockSpec((norb, norb), lambda i: (0, 0))
    final, rfactor = pl.pallas_call(
        mix_kernel,
        grid=(bx * by // piece,),
        out_shape=(jax.ShapeDtypeStruct((norb, bx * by, nz), f32), small[0]),
        in_specs=[block, square, square],
        out_specs=(block, square),
        compiler_params=pltpu.CompilerParams(vmem_limit_bytes=60 << 20),
        name="mix",
    )(back.reshape(norb, bx * by, nz), inverse, upper)
    return (final.reshape(orbitals.shape), rfactor)


def solution(mesh):
    return jax.shard_map(
        functools.partial(per_device, mesh.shape["gx"], mesh.shape["gy"]),
        mesh=mesh,
        in_specs=(P(None, "gx", "gy", None), P("gx", "gy", None)),
        out_specs=(P(None, "gx", "gy", None), P()),
        check_vma=False,
    )
```

```python
import functools
import numpy as np
import jax
import jax.numpy as jnp
from jax import lax
from jax.experimental import pallas as pl
from jax.experimental.pallas import tpu as pltpu
from jax.sharding import PartitionSpec as P

DEGREE = 3
REACH = 6
stencil_weights = (
    -5369.0 / 1800.0,
    12.0 / 7.0,
    -15.0 / 56.0,
    10.0 / 189.0,
    -1.0 / 112.0,
    2.0 / 1925.0,
    -1.0 / 16632.0,
)
grid_spacing = 0.5
filter_low = 4.0
filter_high = 46.0
centre_shift = 0.5 * (filter_high + filter_low)
half_width = 0.5 * (filter_high - filter_low)
scale = -0.5 / grid_spacing**2 / half_width
side_weights = tuple(scale * w for w in stencil_weights)
MESH = pl.DeviceIdType.MESH


def circulant(size):
    matrix = np.zeros((size, size), np.float64)
    for offset in range(1, REACH + 1):
        for i in range(size):
            matrix[i, (i + offset) % size] += side_weights[offset]
            matrix[i, (i - offset) % size] += side_weights[offset]
    return matrix


def split_const(matrix):
    parts, rest = [], matrix
    for _ in range(3):
        part = rest.astype(jnp.bfloat16)
        parts.append(part)
        rest = rest - part.astype(np.float64)
    return parts


def split(value):
    high = value.astype(jnp.bfloat16)
    rest = value - high.astype(jnp.float32)
    mid = rest.astype(jnp.bfloat16)
    low = (rest - mid.astype(jnp.float32)).astype(jnp.bfloat16)
    return high, mid, low


def place(rows):
    gx, gy = lax.axis_index("gx"), lax.axis_index("gy")
    inner = lax.rem(gx, rows)
    return gx - inner, inner, gy


def steps_far_near(rows, n_gy):
    steps = sorted(range(rows), key=lambda j: -min(j, rows - j))
    pairs = [(j, d) for j in steps for d in range(n_gy) if (j, d) != (0, 0)]
    mixed = []
    while pairs:
        mixed.append(pairs.pop(0))
        if pairs:
            mixed.append(pairs.pop())
    return mixed


def greet(rows, n_gy):
    first, inner, gy = place(rows)
    barrier = pltpu.get_barrier_semaphore()
    for j in range(rows):
        for d in range(n_gy):
            if (j, d) != (0, 0):
                who = (first + lax.rem(inner + j, rows), lax.rem(gy + d, n_gy))
                pl.semaphore_signal(barrier, inc=1, device_id=who, device_id_type=MESH)
    pl.semaphore_wait(barrier, rows * n_gy - 1)


def spread(
    rows, n_gy, origin, orb, pot, field, allpot, send, recv, psend, precv, own, meanwhile=None
):
    bx, by = pot.shape[0], pot.shape[1]
    first, inner, gy = place(rows)
    gx_bits, gy_bits = rows.bit_length() - 1, n_gy.bit_length() - 1
    bits = gx_bits + gy_bits
    member = inner * n_gy + gy
    mine = [lax.rem(member // (1 << (bits - 1 - b)), 2) for b in range(bits)]
    brick = field.at[
        pl.ds(origin + inner * bx, bx), pl.ds(pl.multiple_of(gy * by, by), by)
    ]

    def region(done):
        index = [slice(None) if b in done else mine[b] for b in range(bits)]
        return allpot.at[tuple(index[:gx_bits]) + (slice(None),) + tuple(index[gx_bits:])]

    def hop(stage, bit, done):
        t = member + (1 << (bits - 1 - bit)) * (1 - 2 * mine[bit])
        return pltpu.make_async_remote_copy(
            region(done),
            region(done),
            psend.at[stage],
            precv.at[stage],
            device_id=(first + t // n_gy, lax.rem(t, n_gy)),
            device_id_type=MESH,
        )

    plain = list(range(bits))
    swapped = list(plain)
    if bits >= 3:
        swapped[bits - 3], swapped[bits - 2] = bits - 2, bits - 3
    odd = mine[bits - 1] == 1

    def on_hop(stage, act):
        if plain[: stage + 1] == swapped[: stage + 1] or stage == bits - 1:
            act(hop(stage, plain[stage], plain[:stage]))
        else:
            pl.when(jnp.logical_not(odd))(
                lambda: act(hop(stage, plain[stage], plain[:stage]))
            )
            pl.when(odd)(lambda: act(hop(stage, swapped[stage], swapped[:stage])))

    keep = pltpu.make_async_copy(orb.at[member], brick, own.at[0])
    keep_pot = pltpu.make_async_copy(pot, region([]), own.at[1])
    keep.start()
    keep_pot.start()
    greet(rows, n_gy)
    keep_pot.wait()

    order = steps_far_near(rows, n_gy)
    copies = []
    per = -(-len(order) // max(bits, 1))
    for b in range(bits):
        on_hop(b, lambda copy: copy.start())
        for j, d in order[b * per : (b + 1) * per]:
            tx, ty = lax.rem(inner + j, rows), lax.rem(gy + d, n_gy)
            copy = pltpu.make_async_remote_copy(
                orb.at[tx * n_gy + ty],
                brick,
                send.at[j * n_gy + d],
                recv.at[j * n_gy + d],
                device_id=(first + tx, ty),
                device_id_type=MESH,
            )
            copy.start()
            copies.append(copy)
        on_hop(b, lambda copy: copy.wait())
    if meanwhile is not None:
        meanwhile()
    for copy in copies:
        copy.wait()
    keep.wait()


def send_block(rows, n_gy, origin, j, field, out, send, recv, own):
    bx, by = out.shape[1], out.shape[2]
    first, inner, gy = place(rows)
    member = inner * n_gy + gy
    tx = lax.rem(inner + j, rows)
    copies = []
    for d in range(n_gy):
        ty = lax.rem(gy + d, n_gy)
        part = field.at[
            pl.ds(origin + tx * bx, bx), pl.ds(pl.multiple_of(ty * by, by), by)
        ]
        if (j, d) == (0, 0):
            copy = pltpu.make_async_copy(part, out.at[member], own)
        else:
            copy = pltpu.make_async_remote_copy(
                part,
                out.at[member],
                send.at[j * n_gy + d],
                recv.at[j * n_gy + d],
                device_id=(first + tx, ty),
                device_id_type=MESH,
            )
        copy.start()
        copies.append(copy)
    return copies


def block_order(rows):
    steps = sorted(range(1, rows), key=lambda j: -min(j, rows - j))
    mixed = []
    while steps:
        mixed.append(steps.pop(0))
        if steps:
            mixed.append(steps.pop())
    return mixed + [0]


def apply_planes(src, here, count, pot_planes, cz, cy, dst, there, prev):
    ny, nz = src.shape[1], src.shape[2]
    half = cy.shape[1] // 2
    centre = src[pl.ds(here, count)]
    acc = ((pot_planes - centre_shift) * (1.0 / half_width) + 3.0 * side_weights[0]) * centre
    high, mid, low = split(centre.reshape(count * ny, nz))

    def dot(left, right):
        return jnp.dot(left, right, preferred_element_type=jnp.float32)

    def beside(value):
        return jnp.concatenate(
            [value[g : g + half] for g in range(0, count * ny, half)], axis=1
        )

    along = dot(jnp.concatenate([high, mid], axis=1), cz[:, : 2 * nz])
    lines = along[:, :nz] + along[:, nz:]
    lines = lines + dot(jnp.concatenate([low, high], axis=1), cz[:, 2 * nz :])
    high, mid, low = beside(high), beside(mid), beside(low)
    across = dot(cy[: 2 * half], jnp.concatenate([high, mid], axis=0))
    across = across[:half] + across[half:]
    across = across + dot(cy[2 * half :], jnp.concatenate([low, high], axis=0))
    lines = lines + jnp.concatenate(
        [across[:, g : g + nz] for g in range(0, across.shape[1], nz)], axis=0
    )
    for offset in range(1, REACH + 1):
        acc += side_weights[offset] * (
            src[pl.ds(here + offset, count)] + src[pl.ds(here - offset, count)]
        )
    acc += lines.reshape(count, ny, nz)
    if prev is not None:
        acc = 2.0 * acc - prev[pl.ds(here, count)]
    dst[pl.ds(there, count)] = acc


def whole_kernel(
    rows, n_gy, cells, orb, pot, cy_far, cz_far, out, rfac, inverse,
    back, stack, ybuf, xbuf, ysend, yrecv, xsend, xrecv,
    cy_wide, cz_wide, cy, cz, first_buf, second_buf, allpot, send, recv, psend, precv, own, bsend, brecv,
):
    bx, ny, nz = pot.shape[0], first_buf.shape[1], first_buf.shape[2]
    extent = rows * bx
    gx_bits = rows.bit_length() - 1
    fetch = [
        pltpu.make_async_copy(cy_far, cy_wide, own.at[2]),
        pltpu.make_async_copy(cz_far, cz_wide, own.at[3]),
    ]
    for copy in fetch:
        copy.start()

    def fetched():
        for copy in fetch:
            copy.wait()
        cy[...] = cy_wide[...].astype(jnp.bfloat16)
        cz[...] = cz_wide[...].astype(jnp.bfloat16)

    spread(rows, n_gy, REACH, orb, pot, first_buf, allpot, send, recv, psend, precv, own,
           fetched)
    _, inner, _ = place(rows)

    def pot_block(block):
        index = tuple(lax.rem(block // (1 << (gx_bits - 1 - b)), 2) for b in range(gx_bits))
        return allpot[index].reshape(bx, ny, nz)

    def wrap(buf):
        buf[0:REACH] = buf[extent : extent + REACH]
        buf[extent + REACH : extent + 2 * REACH] = buf[REACH : 2 * REACH]

    bufs = (first_buf, second_buf)
    copies = []
    for step in range(1, DEGREE + 1):
        src, other = bufs[(step - 1) % 2], bufs[step % 2]
        wrap(src)
        prev = None if step == 1 else other
        if step < DEGREE:

            def body(block, carry, src=src, other=other, prev=prev):
                at = REACH + block * bx
                apply_planes(src, at, bx, pot_block(block), cz, cy, other, at, prev)
                return carry

            lax.fori_loop(0, rows, body, 0, unroll=True)
        else:
            for j in block_order(rows):
                block = lax.rem(inner + j, rows)
                at = REACH + block * bx
                apply_planes(src, at, bx, pot_block(block), cz, cy, other, at, prev)
                copies += send_block(
                    rows, n_gy, REACH, j, other, back, bsend, brecv, own.at[0]
                )
    for copy in copies:
        copy.wait()
    keep = pltpu.make_async_copy(back, out, own.at[0])
    keep.start()
    flat = back.reshape(back.shape[0] * back.shape[1] * back.shape[2], nz)
    factor(
        rows, n_gy, cells, flat, rfac, inverse, stack, ybuf, xbuf, ysend, yrecv, xsend, xrecv
    )
    keep.wait()


def spread_kernel(rows, n_gy, orb, pot, field, allpot, send, recv, psend, precv, own):
    spread(rows, n_gy, 0, orb, pot, field, allpot, send, recv, psend, precv, own)


def return_kernel(rows, n_gy, field, out, send, recv, own):
    greet(rows, n_gy)
    copies = []
    for j in block_order(rows):
        copies += send_block(rows, n_gy, 0, j, field, out, send, recv, own)
    for copy in copies:
        copy.wait()


def filter_kernel(extent, field, pot, cy, cz, out, first_buf, second_buf):
    origin = REACH * DEGREE
    count = cy.shape[1] // 2 // field.shape[1]
    first_buf[...] = field[...]
    bufs = (first_buf, second_buf)
    for step in range(1, DEGREE + 1):
        src, other = bufs[(step - 1) % 2], bufs[step % 2]
        last = step == DEGREE
        margin = REACH * (DEGREE - step)
        prev = None if step == 1 else other
        dst, base = (out, 0) if last else (other, origin)

        def body(i, carry, src=src, dst=dst, base=base, prev=prev, margin=margin):
            at = i * count - margin
            planes = pot[pl.ds(origin + at, count)]
            apply_planes(src, origin + at, count, planes, cz, cy, dst, base + at, prev)
            return carry

        lax.fori_loop(0, (extent + 2 * margin) // count, body, 0)


def greet_lines(n_gx, n_gy):
    gx, gy = lax.axis_index("gx"), lax.axis_index("gy")
    barrier = pltpu.get_barrier_semaphore()
    for k in range(1, n_gy):
        pl.semaphore_signal(
            barrier, inc=1, device_id=(gx, lax.rem(gy + k, n_gy)), device_id_type=MESH
        )
    for k in range(1, n_gx):
        pl.semaphore_signal(
            barrier, inc=1, device_id=(lax.rem(gx + k, n_gx), gy), device_id_type=MESH
        )
    pl.semaphore_wait(barrier, n_gy + n_gx - 2)


def factor_kernel(n_gx, n_gy, cells, *refs):
    greet_lines(n_gx, n_gy)
    factor(n_gx, n_gy, cells, *refs)


def factor(
    n_gx, n_gy, cells, matrix, rfac, inverse, stack, ybuf, xbuf, ysend, yrecv, xsend, xrecv
):
    gx, gy = lax.axis_index("gx"), lax.axis_index("gy")
    norb = rfac.shape[0]
    nz = matrix.shape[1]
    lines = matrix.shape[0] // norb
    for r in range(lines):
        for p, part in enumerate(split(matrix[pl.ds(r, norb, stride=lines)])):
            stack[p * norb : (p + 1) * norb, r * nz : (r + 1) * nz] = part
    square = lax.dot_general(
        stack[...], stack[...], (((1,), (1,)), ((), ())), preferred_element_type=jnp.float32
    )
    gram = None
    for p, q in ((2, 2), (1, 2), (2, 1), (0, 2), (2, 0), (1, 1), (0, 1), (1, 0), (0, 0)):
        term = square[p * norb : (p + 1) * norb, q * norb : (q + 1) * norb]
        gram = term if gram is None else gram + term
    pack = 128 // norb
    tall = norb // pack
    gram = gram / cells
    gram = jnp.concatenate([gram[i * tall : (i + 1) * tall] for i in range(pack)], axis=1)

    ybuf[gy] = gram
    copies = []
    for k in range(1, n_gy):
        copy = pltpu.make_async_remote_copy(
            ybuf.at[gy],
            ybuf.at[gy],
            ysend.at[k],
            yrecv.at[k],
            device_id=(gx, lax.rem(gy + k, n_gy)),
            device_id_type=MESH,
        )
        copy.start()
        copies.append(copy)
    for copy in copies:
        copy.wait()
    part = ybuf[0]
    for s in range(1, n_gy):
        part = part + ybuf[s]
    xbuf[gx] = part
    copies = []
    for k in range(1, n_gx):
        copy = pltpu.make_async_remote_copy(
            xbuf.at[gx],
            xbuf.at[gx],
            xsend.at[k],
            xrecv.at[k],
            device_id=(lax.rem(gx + k, n_gx), gy),
            device_id_type=MESH,
        )
        copy.start()
        copies.append(copy)
    for copy in copies:
        copy.wait()
    whole = xbuf[0]
    for s in range(1, n_gx):
        whole = whole + xbuf[s]

    row = lax.broadcasted_iota(jnp.int32, (norb, 128), 0)
    col = lax.broadcasted_iota(jnp.int32, (norb, 128), 1)
    whole = jnp.concatenate([whole[:, i * norb : (i + 1) * norb] for i in range(pack)], axis=0)
    whole = jnp.concatenate([whole, jnp.zeros((norb, 128 - norb), jnp.float32)], axis=1)
    table = jnp.where(col == row + norb, 1.0, whole)
    pivots = jnp.zeros((norb, 128), jnp.float32)
    for k in range(norb):
        pivot = table[k : k + 1, k : k + 1]
        pivots = jnp.where(row == k, pivot, pivots)
        ratio = jnp.where(row[:, :1] > k, table[:, k : k + 1] * (1.0 / pivot), 0.0)
        table = table - ratio * table[k : k + 1, :]
    table = table * lax.rsqrt(pivots)
    rfac[...] = jnp.where(row[:, :norb] <= col[:, :norb], table[:, :norb], 0.0)
    inverse[...] = table[:, norb : 2 * norb]


def mix_kernel(bricks, inverse, upper, out, rfac):
    norb, lines, nz = bricks.shape
    rfac[...] = upper[...]
    matrix, mixed_rows = bricks.reshape(norb * lines, nz), out.reshape(norb * lines, nz)
    h, m, l = split(inverse[...])
    left = jnp.concatenate([h, h, h, m, m, l], axis=1)
    for r in range(0, lines, 2):
        both = jnp.concatenate(
            [matrix[pl.ds(r + i, norb, stride=lines)] for i in range(2)], axis=1
        )
        h, m, l = split(both)
        mixed = jnp.dot(
            left,
            jnp.concatenate([h, m, l, h, m, h], axis=0),
            preferred_element_type=jnp.float32,
        )
        for i in range(2):
            mixed_rows[pl.ds(r + i, norb, stride=lines)] = mixed[:, i * nz : (i + 1) * nz]


def per_device(n_gx, n_gy, orbitals, potential):
    norb, bx, by, nz = orbitals.shape
    rows = norb // n_gy
    groups = n_gx // rows
    extent, ny = rows * bx, n_gy * by
    f32 = jnp.float32
    anywhere = pl.BlockSpec(memory_space=pltpu.HBM)
    vmem = pl.BlockSpec(memory_space=pltpu.VMEM)
    dma = pltpu.SemaphoreType.DMA
    gx_bits, gy_bits = rows.bit_length() - 1, n_gy.bit_length() - 1
    bits = gx_bits + gy_bits
    pot_shape = (2,) * gx_bits + (bx,) + (2,) * gy_bits + (by, nz)
    spread_sems = [dma((norb,)), dma((norb,)), dma((bits,)), dma((bits,)), dma((4,))]
    brick_shape = jax.ShapeDtypeStruct((norb, bx, by, nz), f32)

    yh, ym, yl = split_const(np.kron(np.eye(4), circulant(ny)))
    cy = jnp.asarray(np.block([[yh, yh], [ym, ym], [yh, yl]]), f32)
    zh, zm, zl = split_const(circulant(nz))
    cz = jnp.asarray(np.block([[zh, zm, zh], [zh, zm, zl]]), f32)

    cells = float(bx * by * nz * n_gx * n_gy)
    small = (jax.ShapeDtypeStruct((norb, norb), f32),) * 2
    factor_scratch = [
        pltpu.VMEM((3 * norb, bx * by * nz), jnp.bfloat16),
        pltpu.VMEM((n_gy, norb * norb // 128, 128), f32),
        pltpu.VMEM((n_gx, norb * norb // 128, 128), f32),
        dma((n_gy,)),
        dma((n_gy,)),
        dma((n_gx,)),
        dma((n_gx,)),
    ]

    if groups == 1:
        planes = extent + 2 * REACH
        back, upper, inverse = pl.pallas_call(
            functools.partial(whole_kernel, rows, n_gy, cells),
            out_shape=(brick_shape,) + small,
            in_specs=[anywhere] * 4,
            out_specs=(anywhere, vmem, vmem),
            scratch_shapes=[pltpu.VMEM(brick_shape.shape, f32)]
            + factor_scratch
            + [
                pltpu.VMEM(cy.shape, f32),
                pltpu.VMEM(cz.shape, f32),
                pltpu.VMEM(cy.shape, jnp.bfloat16),
                pltpu.VMEM(cz.shape, jnp.bfloat16),
                pltpu.VMEM((planes, ny, nz), f32),
                pltpu.VMEM((planes, ny, nz), f32),
                pltpu.VMEM(pot_shape, f32),
            ]
            + spread_sems
            + [dma((norb,)), dma((norb,))],
            compiler_params=pltpu.CompilerParams(
                collective_id=0, has_side_effects=True, vmem_limit_bytes=60 << 20
            ),
            name="spread_filter_return_factor",
        )(orbitals, potential, cy, cz)
    else:
        field, allpot = pl.pallas_call(
            functools.partial(spread_kernel, rows, n_gy),
            out_shape=(
                jax.ShapeDtypeStruct((extent, ny, nz), f32),
                jax.ShapeDtypeStruct(pot_shape, f32),
            ),
            in_specs=[anywhere] * 2,
            out_specs=(anywhere, anywhere),
            scratch_shapes=spread_sems,
            compiler_params=pltpu.CompilerParams(collective_id=0, has_side_effects=True),
            name="spread",
        )(orbitals, potential)
        halo = REACH * DEGREE
        up = [(i, (i + rows) % n_gx) for i in range(n_gx)]
        down = [(t, s) for s, t in up]

        def widen(block):
            low = lax.ppermute(block[extent - halo :], "gx", up)
            high = lax.ppermute(block[:halo], "gx", down)
            return jnp.concatenate([low, block, high], axis=0)

        planes = extent + 2 * halo
        filtered = pl.pallas_call(
            functools.partial(filter_kernel, extent),
            out_shape=jax.ShapeDtypeStruct((extent, ny, nz), f32),
            in_specs=[vmem] * 4,
            out_specs=vmem,
            scratch_shapes=[pltpu.VMEM((planes, ny, nz), f32)] * 2,
            compiler_params=pltpu.CompilerParams(vmem_limit_bytes=24 << 20),
            name="filter",
        )(
            widen(field),
            widen(allpot.reshape(extent, ny, nz)),
            cy.astype(jnp.bfloat16),
            cz.astype(jnp.bfloat16),
        )
        back = pl.pallas_call(
            functools.partial(return_kernel, rows, n_gy),
            out_shape=brick_shape,
            in_specs=[anywhere],
            out_specs=anywhere,
            scratch_shapes=[dma((norb,)), dma((norb,)), dma],
            compiler_params=pltpu.CompilerParams(collective_id=1, has_side_effects=True),
            name="hand_back",
        )(filtered)

        upper, inverse = pl.pallas_call(
            functools.partial(factor_kernel, n_gx, n_gy, cells),
            out_shape=small,
            in_specs=[vmem],
            out_specs=(vmem, vmem),
            scratch_shapes=factor_scratch,
            compiler_params=pltpu.CompilerParams(
                collective_id=2, has_side_effects=True, vmem_limit_bytes=24 << 20
            ),
            name="factor",
        )(back.reshape(norb * bx * by, nz))

    final, rfactor = pl.pallas_call(
        mix_kernel,
        out_shape=(jax.ShapeDtypeStruct((norb, bx * by, nz), f32), small[0]),
        in_specs=[vmem] * 3,
        out_specs=(vmem, vmem),
        compiler_params=pltpu.CompilerParams(vmem_limit_bytes=24 << 20),
        name="mix",
    )(back.reshape(norb, bx * by, nz), inverse, upper)
    return (final.reshape(orbitals.shape), rfactor)


def solution(mesh):
    return jax.shard_map(
        functools.partial(per_device, mesh.shape["gx"], mesh.shape["gy"]),
        mesh=mesh,
        in_specs=(P(None, "gx", "gy", None), P("gx", "gy", None)),
        out_specs=(P(None, "gx", "gy", None), P()),
        check_vma=False,
    )
```
